512 devices in a mesh: grp: 8 (over y_lo, x), dev: 64 (over z, y_hi, core).
Axes of the slice: x: 4, y: 8 (y_hi: 4, y_lo: 2; y = y_hi * 2 + y_lo), z: 8, core: 2. Of those that a mesh axis runs over, the one named last changes fastest.
Arguments:
- e_field: float32 [3, 64, 512, 640], P(None, 'grp', 'dev'), may hold values from -6 to 6
- h_field: float32 [3, 64, 512, 640], P(None, 'grp', 'dev'), may hold values from -6 to 6
- polar: float32 [2, 3, 64, 512, 640], P(None, None, 'grp', 'dev'), may hold values from -3 to 3
- material: int32 [64, 512], P('grp', 'dev'), may hold values from 0 to 3, as said below
- eps_table: float32 [4], replicated, may hold values from 1 to 4
- loss_table: float32 [4], replicated, may hold values from 0.02 to 0.4
- lorentz: float32 [3], replicated, may hold values from 0.3 to 1.2
- freqs: float32 [4], replicated, may hold values from 0.3 to 1.5
Outputs:
- e_final: float32 [3, 64, 512, 640], P(None, 'grp', 'dev')
- h_final: float32 [3, 64, 512, 640], P(None, 'grp', 'dev')
- polar_final: float32 [2, 3, 64, 512, 640], P(None, None, 'grp', 'dev')
- spectrum: float32 [4, 2, 3, 8, 512, 640], P(None, None, None, 'grp', 'dev')
The draws below stay inside these ranges and needn't reach their ends.
Inputs may be any that keep to these rules, and one draw needn't show every extreme that they name: `material`: kind 3 names at most 32 of the 64 rows of one device's block, and exactly 32 rows in some device's block.
All inputs are finite; a program needn't handle non-finite values.
Results may differ from the reference program's by a relative error of at most 0.00002.
Values sent between devices are 32-bit elements; how exact they have to be, the bound alone decides.
No kernel may reach another device: no remote copies, remote signals or barrier semaphores. Data moves between devices by JAX's collectives and lax.ppermute only.
A program may use at most 64 MiB of HBM per device.

```python
import jax
import jax.numpy as jnp
from jax import lax

CZ = 8
CX = 8
NY = 640
STEPS = 4
FREQS = 4
NZ = 64
NX = 512
PLANES = 8
LROWS = 32


def draw_material(key, part):
    key = jax.random.fold_in(key, 11)
    blocks_z = NZ // CZ
    blocks_x = NX // CX
    blocks = blocks_z * blocks_x
    rows = CZ * CX
    key_count, key_full, key_order, key_other = jax.random.split(key, 4)
    counts = jax.random.randint(key_count, (blocks,), 0, LROWS + 1)
    chosen = jax.random.randint(key_full, (), 0, blocks)
    counts = jnp.where(jnp.arange(blocks) == chosen, LROWS, counts)
    order_keys = jax.random.split(key_order, blocks)
    orders = jax.vmap(lambda single: jax.random.permutation(single, rows))(order_keys)
    others = jax.random.randint(key_other, (blocks, rows), 0, 3)
    kinds = jnp.where(orders < counts[:, None], 3, others)
    kinds = kinds.reshape(blocks_z, blocks_x, CZ, CX).transpose(0, 2, 1, 3).reshape(NZ, NX)
    return kinds.astype(jnp.int32)


def shard_levels(rng, extent, pieces, low, high):
    def one(dim, shards_of):
        heights = jax.random.uniform(jax.random.fold_in(jax.random.fold_in(rng, 6), dim), (shards_of,), jnp.float32, low / len(pieces), high / len(pieces))
        return jnp.repeat(jnp.exp(heights), extent[dim] // shards_of).reshape((-1,) + (1,) * (len(extent) - dim - 1))

    factor_of = one(*pieces[0])
    for cut in pieces[1:]:
        factor_of = factor_of * one(*cut)
    return factor_of


def bell_draw(own_key, shape, deviation, bound, cuts=(), kind=jnp.bfloat16):
    loudness = shard_levels(own_key, shape, cuts, -0.22, 0.18) if cuts else 1.0
    entries = jax.random.normal(own_key, shape, jnp.float32) * deviation * loudness
    return jnp.minimum(jnp.maximum(entries, -bound), bound).astype(kind)


def setup_inputs(seed: int = 0) -> dict:
    arg_keys = jax.random.split(jax.random.key(seed), 9)
    e_field = bell_draw(arg_keys[0], (3, NZ, NX, NY), 1.0, 6.0, ((1, 8), (2, 64)), jnp.float32)
    h_field = bell_draw(arg_keys[1], (3, NZ, NX, NY), 1.0, 6.0, ((1, 8), (2, 64)), jnp.float32)
    polar = bell_draw(arg_keys[2], (2, 3, NZ, NX, NY), 0.5, 3.0, ((2, 8), (3, 64)), jnp.float32)
    material = draw_material(jax.random.fold_in(arg_keys[8], 71), 0)
    eps_table = jnp.clip(jax.random.uniform(arg_keys[4], (4,), jnp.float32, 1.0, 4.0), 1.0, 4.0)
    loss_table = jnp.clip(jax.random.uniform(arg_keys[5], (4,), jnp.float32, 0.02, 0.4), 0.02, 0.4)
    lorentz = jnp.clip(jax.random.uniform(arg_keys[6], (3,), jnp.float32, 0.3, 1.2), 0.3, 1.2)
    freqs = jnp.clip(jax.random.uniform(arg_keys[7], (FREQS,), jnp.float32, 0.3, 1.5), 0.3, 1.5)
    return {"e_field": e_field, "h_field": h_field, "polar": polar, "material": material, "eps_table": eps_table, "loss_table": loss_table, "lorentz": lorentz, "freqs": freqs}


COURANT = 0.5


def lookup(material, table):
    total = jnp.zeros(material.shape, jnp.float32)
    for species in range(4):
        total = total + jnp.where(material == species, table[species], jnp.float32(0.0))
    return total[..., None]


def ahead(field, axis, border):
    inner = lax.slice_in_dim(field, 1, field.shape[axis], axis=axis)
    return jnp.concatenate([inner, border], axis=axis)


def behind(field, axis, border):
    inner = lax.slice_in_dim(field, 0, field.shape[axis] - 1, axis=axis)
    return jnp.concatenate([border, inner], axis=axis)


def curl_ahead(fields, upper_z, upper_x):
    border = jnp.zeros(fields.shape[1:3] + (1,), jnp.float32)
    first, second, third = fields[0], fields[1], fields[2]
    return jnp.stack([
        (ahead(third, 2, border) - third) - (ahead(second, 0, upper_z[1]) - second),
        (ahead(first, 0, upper_z[0]) - first) - (ahead(third, 1, upper_x[1]) - third),
        (ahead(second, 1, upper_x[0]) - second) - (ahead(first, 2, border) - first)])


def curl_behind(fields, lower_z, lower_x):
    border = jnp.zeros(fields.shape[1:3] + (1,), jnp.float32)
    first, second, third = fields[0], fields[1], fields[2]
    return jnp.stack([
        (third - behind(third, 2, border)) - (second - behind(second, 0, lower_z[1])),
        (first - behind(first, 0, lower_z[0])) - (third - behind(third, 1, lower_x[1])),
        (second - behind(second, 1, lower_x[0])) - (first - behind(first, 2, border))])


def polar_step(current, previous, driver, params):
    resonance = params[0]
    damper = params[1]
    strength = params[2]
    return ((2.0 - resonance * resonance) * current - (1.0 - 0.5 * damper) * previous
            + strength * resonance * resonance * driver) / (1.0 + 0.5 * damper)


def reference(e_field, h_field, polar, material, eps_table, loss_table, lorentz, freqs):
    damping = lookup(material, loss_table)
    permittivity = lookup(material, eps_table)
    retain = (1.0 - damping) / (1.0 + damping)
    h_gain = COURANT / (1.0 + damping)
    e_gain = COURANT / (permittivity * (1.0 + damping))
    active = (material == 3)[..., None]
    zero_z = jnp.zeros((2, 1) + e_field.shape[2:], jnp.float32)
    zero_x = jnp.zeros((2, e_field.shape[1], 1, e_field.shape[3]), jnp.float32)
    current = polar[0]
    previous = polar[1]
    spectrum = jnp.zeros((FREQS, 2, 3, PLANES) + e_field.shape[2:], jnp.float32)
    for step in range(STEPS):
        h_field = retain * h_field - h_gain * curl_ahead(e_field, zero_z, zero_x)
        updated = jnp.where(active, polar_step(current, previous, e_field, lorentz), current)
        previous = jnp.where(active, current, previous)
        e_field = retain * e_field + e_gain * curl_behind(h_field, zero_z, zero_x) - (updated - current) / permittivity
        current = updated
        angles = freqs * float(step + 1)
        weights = jnp.stack([jnp.cos(angles), -jnp.sin(angles)], axis=1)
        monitor = e_field[:, CZ // 2::CZ]
        spectrum = spectrum + weights[:, :, None, None, None, None] * monitor[None, None]
    return e_field, h_field, jnp.stack([current, previous]), spectrum
```

```python
import functools

import jax
import jax.numpy as jnp
from jax import lax
from jax.experimental import pallas as pl
from jax.experimental.pallas import tpu as pltpu
from jax.sharding import PartitionSpec as P


STEPS = 4
FREQS = 4
COURANT = 0.5
N = 8
NY = 640
LANES = 128

ROWS = 17
Z0 = 5

X_TILES = 13
Z_TILES = 19


def ladder(first, count, start, way):
    return [(first + i, start + way * j) for i in range(count) for j in range(count - i)]


def ray_rows(entries, tile):
    out = {}
    for c in range(2):
        for kind, n, place in entries:
            k = len(out)
            out[(kind, n, c, place)] = (tile + k // 8, k % 8)
    return out


HX = ray_rows([("ze", n, x) for n, x in ladder(0, 3, 0, 1)] + [("zh", n, x) for n, x in ladder(1, 3, 0, 1)], 8)
LX = ray_rows([("ze", n, x) for n, x in ladder(0, 4, 7, -1)] + [("zh", n, x) for n, x in ladder(1, 3, 7, -1)], 8)
HZ = ray_rows(
    [("zeh", n, x) for n, x in ladder(0, 3, 0, 1)]
    + [("zel", n, x) for n, x in ladder(0, 4, 7, -1)]
    + [("xe", n, z) for n, z in ladder(0, 3, 0, 1)]
    + [("xh", n, z) for n, z in ladder(1, 2, 0, 1)]
    + [("xhl", n, z) for n, z in ladder(1, 3, 0, 1)]
    + [("xeh", n, z) for n, z in ladder(0, 3, 0, 1)],
    9,
)
LZ = ray_rows(
    [("zhh", n, x) for n, x in ladder(1, 3, 0, 1)]
    + [("zhl", n, x) for n, x in ladder(1, 3, 7, -1)]
    + [("xe", n, z) for n, z in ladder(0, 3, 7, -1)]
    + [("xh", n, z) for n, z in ladder(1, 3, 7, -1)]
    + [("xhl", n, z) for n, z in ladder(1, 3, 7, -1)]
    + [("xeh", n, z) for n, z in ladder(0, 4, 7, -1)],
    9,
)


def slot_e(n, c):
    return 2 * n + c


def slot_h(n, c):
    return 2 * (n - 1) + c


def wide(tile):
    return jnp.concatenate([tile] * (NY // LANES), axis=1)


def sublane(shape):
    return lax.broadcasted_iota(jnp.int32, shape, 0)


def lane(shape):
    return lax.broadcasted_iota(jnp.int32, shape, 1)


def y_ahead(v):
    r = pltpu.roll(v, NY - 1, 1)
    last = r[:, NY - LANES :]
    return jnp.concatenate([r[:, : NY - LANES], jnp.where(lane(last.shape) == LANES - 1, 0.0, last)], axis=1)


def y_behind(v):
    r = pltpu.roll(v, 1, 1)
    first = r[:, :LANES]
    return jnp.concatenate([jnp.where(lane(first.shape) == 0, 0.0, first), r[:, LANES:]], axis=1)


def x_up(v):
    return pltpu.roll(v, N - 1, 0)


def x_down(v):
    return pltpu.roll(v, 1, 0)


def kind_tables(eps_ref, loss_ref):
    out = []
    for k in range(4):
        damping = jnp.full((N, LANES), loss_ref[k], jnp.float32)
        permittivity = jnp.full((N, LANES), eps_ref[k], jnp.float32)
        scale = 1.0 / (1.0 + damping)
        inverse = 1.0 / permittivity
        out.append(((1.0 - damping) * scale, COURANT * scale, COURANT * scale * inverse, inverse))
    return out


def row_coefficients(kind, tables):
    out = []
    for j in range(4):
        total = jnp.zeros((N, LANES), jnp.float32)
        for k in range(4):
            total = jnp.where(kind == k + 1.0, tables[k][j], total)
        out.append(total)
    out.append(jnp.where(kind == 4.0, 1.0, 0.0))
    return out


def polar_scalars(lorentz_ref):
    shape = (N, LANES)
    a = jnp.full(shape, lorentz_ref[0], jnp.float32)
    g = jnp.full(shape, lorentz_ref[1], jnp.float32)
    s = jnp.full(shape, lorentz_ref[2], jnp.float32)
    scale = 1.0 / (1.0 + 0.5 * g)
    return (1.0 - a * a - 0.5 * g) * scale, (1.0 - 0.5 * g) * scale, s * a * a * scale


def own_kinds(material_ref):
    sub = sublane((N, LANES))
    out = []
    for z in range(N):
        kind = jnp.zeros((N, LANES), jnp.int32)
        for x in range(N):
            kind = jnp.where(sub == x, material_ref[z, x] + 1, kind)
        out.append(kind.astype(jnp.float32))
    return out


def e_update(curl, e, a, b, k, polar):
    retain, _, e_gain, inverse, active = k
    p, q, r = polar
    moved = active * (p * a - q * b + r * e)
    e_new = retain * e + e_gain * curl - inverse * moved
    return e_new, jnp.where(active > 0.5, a + moved, b)


def alone_kernel(
    e_hbm, h_hbm, p_hbm, material, eps, loss, lorentz, m0, m1, ze_out, zh_out, e, h, a, b, msg, ze, zh, coef, sems
):
    par = lax.rem(lax.axis_index("dev"), 2)
    to_high = par
    to_low = 1 - par
    copies = [
        pltpu.make_async_copy(e_hbm, e.at[:, 0:N], sems.at[0]),
        pltpu.make_async_copy(h_hbm, h.at[:, 1 : N + 1], sems.at[1]),
        pltpu.make_async_copy(p_hbm.at[0], a, sems.at[2]),
        pltpu.make_async_copy(p_hbm.at[1], b, sems.at[3]),
    ]
    for copy in copies:
        copy.start()
    none = jnp.zeros((N, NY), jnp.float32)
    for c in range(3):
        e[c, N] = none
        h[c, 0] = none
    tables = kind_tables(eps, loss)
    polar = [wide(v) for v in polar_scalars(lorentz)]
    ln = lane((N, LANES))
    packed = jnp.zeros((N, LANES), jnp.float32)
    for z, kind in enumerate(own_kinds(material)):
        packed = jnp.where(ln == z, kind, packed)
        for j, v in enumerate(row_coefficients(kind, tables)):
            coef[j, z] = v
    for s in range(2):
        msg[s, 12] = wide(packed)
    for copy in copies:
        copy.wait()

    @pl.loop(0, N)
    def _(z):
        for c in range(2):
            msg[to_low, z, pl.ds(slot_e(0, c), 1), :] = e[1 + c, z, 0:1, :]

    for c in range(2):
        ze[slot_e(0, c)] = e[c, 0]
    sub = sublane((N, NY))
    top = sub == N - 1
    bottom = sub == 0

    for n in range(1, STEPS + 1):
        old, new = (a, b) if n % 2 == 1 else (b, a)

        @pl.loop(0, N)
        def _(z):
            k = [wide(coef[j, z]) for j in range(5)]
            retain, h_gain = k[0], k[1]
            ex, ey, ez = (e[c, z] for c in range(3))
            e1x, e1y = (e[c, z + 1] for c in range(2))
            xa_y = jnp.where(top, 0.0, x_up(ey))
            xa_z = jnp.where(top, 0.0, x_up(ez))
            hx = retain * h[0, z + 1] - h_gain * ((y_ahead(ez) - ez) - (e1y - ey))
            hy = retain * h[1, z + 1] - h_gain * ((e1x - ex) - (xa_z - ez))
            hz = retain * h[2, z + 1] - h_gain * ((xa_y - ey) - (y_ahead(ex) - ex))
            h[0, z + 1] = hx
            h[1, z + 1] = hy
            h[2, z + 1] = hz
            msg[to_high, z, pl.ds(slot_h(n, 0), 1), :] = hy[N - 1 : N, :]
            msg[to_high, z, pl.ds(slot_h(n, 1), 1), :] = hz[N - 1 : N, :]
            if n < STEPS:
                lx, ly = (h[c, z] for c in range(2))
                xb_y = jnp.where(bottom, 0.0, x_down(hy))
                xb_z = jnp.where(bottom, 0.0, x_down(hz))
                curls = (
                    (hz - y_behind(hz)) - (hy - ly),
                    (hx - lx) - (hz - xb_z),
                    (hy - xb_y) - (hx - y_behind(hx)),
                )
                for c, (curl, field) in enumerate(zip(curls, (ex, ey, ez))):
                    e_new, p_new = e_update(curl, field, old[c, z], new[c, z], k, polar)
                    e[c, z] = e_new
                    new[c, z] = p_new
                    if c:
                        msg[to_low, z, pl.ds(slot_e(n, c - 1), 1), :] = e_new[0:1, :]

        for c in range(2):
            zh[slot_h(n, c)] = h[c, N]
            if n < STEPS:
                ze[slot_e(n, c)] = e[c, 0]

    for rays, to in ((HX, to_low), (LX, to_high)):
        for (kind, n, c, x), (tile, row) in rays.items():
            source = ze.at[slot_e(n, c)] if kind == "ze" else zh.at[slot_h(n, c)]
            msg[to, tile, row : row + 1, :] = source[x : x + 1, :]
    copies = [
        pltpu.make_async_copy(msg.at[0], m0, sems.at[0]),
        pltpu.make_async_copy(msg.at[1], m1, sems.at[1]),
        pltpu.make_async_copy(ze, ze_out, sems.at[2]),
        pltpu.make_async_copy(zh, zh_out, sems.at[3]),
    ]
    for copy in copies:
        copy.start()
    for copy in copies:
        copy.wait()


def forward_kernel(m0, m1, r0, r1, ze_in, zh_in, q0, q1, own, got, msg, sems):
    par = lax.rem(lax.axis_index("dev"), 2)
    to_high = lax.rem(lax.axis_index("grp"), 2)
    to_low = 1 - to_high
    copies = [
        pltpu.make_async_copy(m0, own.at[0], sems.at[0]),
        pltpu.make_async_copy(m1, own.at[1], sems.at[1]),
        pltpu.make_async_copy(r0, got.at[0], sems.at[2]),
        pltpu.make_async_copy(r1, got.at[1], sems.at[3]),
        pltpu.make_async_copy(ze_in, msg.at[to_low, 0:8], sems.at[4]),
        pltpu.make_async_copy(zh_in, msg.at[to_high, 0:8], sems.at[5]),
    ]
    for copy in copies:
        copy.start()
    for copy in copies:
        copy.wait()
    high, low = got.at[par], got.at[1 - par]
    mine_e, mine_h = own.at[1 - par], own.at[par]
    ghost = jnp.where(sublane((N, LANES)) < 4, high[12, :, 0:LANES], low[12, :, 0:LANES])
    packed = jnp.concatenate([own[0, 12, :, 0:LANES], ghost] + [ghost] * 3, axis=1)
    for s in range(2):
        msg[s, 8] = packed
    for rays, to in ((HZ, to_low), (LZ, to_high)):
        for (kind, n, c, place), (tile, row) in rays.items():
            if kind in ("zeh", "zhh"):
                t, r = HX[(kind[:2], n, c, place)]
                value = high[t, r : r + 1, :]
            elif kind in ("zel", "zhl"):
                t, r = LX[(kind[:2], n, c, place)]
                value = low[t, r : r + 1, :]
            else:
                r = slot_e(n, c) if kind[:2] == "xe" else slot_h(n, c)
                source = {"xe": mine_e, "xh": mine_h, "xeh": high, "xhl": low}[kind]
                value = source[place, r : r + 1, :]
            msg[to, tile, row : row + 1, :] = value
    copies = [
        pltpu.make_async_copy(msg.at[0], q0, sems.at[0]),
        pltpu.make_async_copy(msg.at[1], q1, sems.at[1]),
    ]
    for copy in copies:
        copy.start()
    for copy in copies:
        copy.wait()


def together_kernel(
    e_hbm, h_hbm, p_hbm, r0, r1, g0, g1, material, eps, loss, lorentz, weights,
    e_out, h_out, p_out, s_out,
    e, h, a, b, gx, gz, xe_hi, xe_lo, xh_lo, xh_hi, ze_hi, ze_lo, zh_lo, zh_hi, coef, spectrum, sems,
):
    par = lax.rem(lax.axis_index("dev"), 2)
    gpar = lax.rem(lax.axis_index("grp"), 2)
    mine = pl.ds(Z0, N)
    fields = [
        pltpu.make_async_copy(e_hbm, e.at[:, mine, 0], sems.at[0]),
        pltpu.make_async_copy(h_hbm, h.at[:, mine, 0], sems.at[1]),
        pltpu.make_async_copy(p_hbm.at[0], a.at[:, mine, 0], sems.at[2]),
        pltpu.make_async_copy(p_hbm.at[1], b.at[:, mine, 0], sems.at[3]),
        pltpu.make_async_copy(r0, gx.at[0], sems.at[4]),
        pltpu.make_async_copy(r1, gx.at[1], sems.at[5]),
        pltpu.make_async_copy(g0, gz.at[0], sems.at[6]),
        pltpu.make_async_copy(g1, gz.at[1], sems.at[7]),
    ]
    for copy in fields:
        copy.start()
    none = jnp.zeros((N, NY), jnp.float32)

    @pl.loop(0, ROWS)
    def _(z):
        for field in (e, h, a, b):
            for c in range(3):
                field[c, z, 1] = none
        for table in (xe_hi, xe_lo, xh_lo, xh_hi):
            table[z] = none

    for z in (*range(Z0), *range(Z0 + N, ROWS)):
        for field in (e, h, a, b):
            for c in range(3):
                field[c, z, 0] = none
    for i in range(2 * STEPS):
        ze_hi[i, 1] = none
        zh_lo[i, 1] = none
        ze_lo[i] = none
        zh_hi[i] = none

    tables = kind_tables(eps, loss)
    polar = [wide(v) for v in polar_scalars(lorentz)]
    for z, kind in enumerate(own_kinds(material)):
        for j, v in enumerate(row_coefficients(kind, tables)):
            coef[j, Z0 + z, 0] = v
    for copy in fields:
        copy.wait()

    high, low = gx.at[par], gx.at[1 - par]
    above, below = gz.at[gpar], gz.at[1 - gpar]
    sub = sublane((N, LANES))
    side = jnp.where(sub < 3, high[12, :, 0:LANES], jnp.where(sub > 3, low[12, :, 0:LANES], 0.0))
    for z in range(-4, N + 3):
        if z < 0 or z >= N:
            tile = below[8] if z < 0 else above[8]
            at = z % N
            both = [tile[:, at : at + 1], tile[:, LANES + at : LANES + at + 1]]
        else:
            both = [None, side[:, z : z + 1]]
        for half, column in enumerate(both):
            if column is None:
                continue
            kind = jnp.broadcast_to(column, (N, LANES))
            if half:
                kind = jnp.where(sub == 3, 0.0, kind)
            for j, v in enumerate(row_coefficients(kind, tables)):
                coef[j, Z0 + z, half] = v

    for z in range(N):
        xe_hi[Z0 + z] = high[z]
        xh_lo[Z0 + z] = low[z]
    for i in range(2 * STEPS):
        ze_hi[i, 0] = above[i]
        zh_lo[i, 0] = below[i]
    for source, rays in ((high, HX), (low, LX)):
        for (kind, n, c, x), (tile, row) in rays.items():
            target = ze_lo.at[slot_e(n, c)] if kind == "ze" else zh_hi.at[slot_h(n, c)]
            target[x : x + 1, :] = source[tile, row : row + 1, :]
    for source, rays, origin in ((above, HZ, Z0 + N), (below, LZ, Z0 - N)):
        for (kind, n, c, place), (tile, row) in rays.items():
            value = source[tile, row : row + 1, :]
            if kind[0] == "z":
                target = ze_hi.at[slot_e(n, c), 1] if kind[1] == "e" else zh_lo.at[slot_h(n, c), 1]
                target[place : place + 1, :] = value
            else:
                r = slot_e(n, c) if kind[1] == "e" else slot_h(n, c)
                target = {"xe": xe_lo, "xh": xh_hi, "xeh": xe_hi, "xhl": xh_lo}[kind]
                target[origin + place, r : r + 1, :] = value

    sub = sublane((N, NY))
    top = sub == N - 1
    bottom = sub == 0

    def across(v, shift, edge, s0, s1):
        v0, v1 = shift(v[0]), shift(v[1])
        return jnp.where(edge, v1 + s0, v0), jnp.where(edge, v0 + s1, v1)

    for n in range(1, STEPS + 1):
        old, new = (a, b) if n % 2 == 1 else (b, a)

        @pl.loop(Z0 - (5 - n), Z0 + N + (4 - n))
        def _(z):
            def rows(table, r):
                return [jnp.broadcast_to(table[z, r + c : r + c + 1, :], (N, NY)) for c in range(2)]

            def k_of(j, half):
                return wide(coef[j, z, half])

            ey = [e[1, z, half] for half in range(2)]
            ez = [e[2, z, half] for half in range(2)]
            s0 = rows(xe_hi, slot_e(n - 1, 0))
            s1 = rows(xe_lo, slot_e(n - 1, 0))
            xa_y = across(ey, x_up, top, s0[0], s1[0])
            xa_z = across(ez, x_up, top, s0[1], s1[1])
            for half in range(2):
                retain, h_gain = k_of(0, half), k_of(1, half)
                ex = e[0, z, half]
                e1x, e1y = e[0, z + 1, half], e[1, z + 1, half]
                h[0, z, half] = retain * h[0, z, half] - h_gain * ((y_ahead(ez[half]) - ez[half]) - (e1y - ey[half]))
                h[1, z, half] = retain * h[1, z, half] - h_gain * ((e1x - ex) - (xa_z[half] - ez[half]))
                h[2, z, half] = retain * h[2, z, half] - h_gain * ((xa_y[half] - ey[half]) - (y_ahead(ex) - ex))

            def h_border(half, sx, sy):
                h_gain = k_of(1, half)
                h[0, z, half] = h[0, z, half] + h_gain * sy
                h[1, z, half] = h[1, z, half] - h_gain * sx

            i = slot_e(n - 1, 0)

            @pl.when(z == Z0 + N - 1)
            def _():
                for half in range(2):
                    h_border(half, ze_hi[i, half], ze_hi[i + 1, half])

            @pl.when(z == Z0 - 1)
            def _():
                h_border(1, ze_lo[i], ze_lo[i + 1])

            hy = [h[1, z, half] for half in range(2)]
            hz = [h[2, z, half] for half in range(2)]
            j = slot_h(n, 0)
            s0 = rows(xh_lo, j)
            s1 = rows(xh_hi, j)
            xb_y = across(hy, x_down, bottom, s0[0], s1[0])
            xb_z = across(hz, x_down, bottom, s0[1], s1[1])
            halves = range(2 if n < STEPS else 1)
            for half in halves:
                k = [k_of(m, half) for m in range(5)]
                hx = h[0, z, half]
                lx, ly = h[0, z - 1, half], h[1, z - 1, half]
                curls = (
                    (hz[half] - y_behind(hz[half])) - (hy[half] - ly),
                    (hx - lx) - (hz[half] - xb_z[half]),
                    (hy[half] - xb_y[half]) - (hx - y_behind(hx)),
                )
                for c in range(3):
                    e_new, p_new = e_update(curls[c], e[c, z, half], old[c, z, half], new[c, z, half], k, polar)
                    e[c, z, half] = e_new
                    new[c, z, half] = p_new

            def e_border(half, sx, sy):
                e_gain = k_of(2, half)
                e[0, z, half] = e[0, z, half] + e_gain * sy
                e[1, z, half] = e[1, z, half] - e_gain * sx

            @pl.when(z == Z0)
            def _():
                for half in halves:
                    e_border(half, zh_lo[j, half], zh_lo[j + 1, half])

            @pl.when(z == Z0 + N)
            def _():
                for half in halves[1:]:
                    e_border(half, zh_hi[j], zh_hi[j + 1])

        for f in range(FREQS):
            for q in range(2):
                for c in range(3):
                    term = weights[n - 1, f, q] * e[c, Z0 + N // 2, 0]
                    spectrum[f, q, c, 0] = term if n == 1 else spectrum[f, q, c, 0] + term

    outs = [
        pltpu.make_async_copy(e.at[:, mine, 0], e_out, sems.at[0]),
        pltpu.make_async_copy(h.at[:, mine, 0], h_out, sems.at[1]),
        pltpu.make_async_copy(a.at[:, mine, 0], p_out.at[0], sems.at[2]),
        pltpu.make_async_copy(b.at[:, mine, 0], p_out.at[1], sems.at[3]),
        pltpu.make_async_copy(spectrum, s_out, sems.at[4]),
    ]
    for copy in outs:
        copy.start()
    for copy in outs:
        copy.wait()


ANY = pl.BlockSpec(memory_space=pl.ANY)
SMEM = pl.BlockSpec(memory_space=pltpu.SMEM)


def f32(*shape):
    return jax.ShapeDtypeStruct(shape, jnp.float32)


def vmem(*shape):
    return pltpu.VMEM(shape, jnp.float32)


def params():
    return pltpu.CompilerParams(vmem_limit_bytes=40 * 1024 * 1024)


def swap(block, axis, parity):
    size = lax.axis_size(axis)
    route = []
    for i in range(parity, size - 1, 2):
        route += [(i, i + 1), (i + 1, i)]
    return lax.ppermute(block, axis, route)


def on_device(e_field, h_field, polar, material, eps_table, loss_table, lorentz, freqs):
    plane = (2 * STEPS, N, NY)
    m0, m1, ze, zh = pl.pallas_call(
        alone_kernel,
        out_shape=[f32(X_TILES, N, NY), f32(X_TILES, N, NY), f32(*plane), f32(*plane)],
        in_specs=[ANY] * 3 + [SMEM] * 4,
        out_specs=[ANY] * 4,
        scratch_shapes=[
            vmem(3, N + 1, N, NY), vmem(3, N + 1, N, NY), vmem(3, N, N, NY), vmem(3, N, N, NY),
            vmem(2, X_TILES, N, NY), vmem(*plane), vmem(*plane), vmem(5, N, N, LANES), pltpu.SemaphoreType.DMA((4,)),
        ],
        compiler_params=params(),
        name="alone",
    )(e_field, h_field, polar, material, eps_table, loss_table, lorentz)
    r1 = swap(m1, "dev", 1)
    r0 = swap(m0, "dev", 0)
    q0, q1 = pl.pallas_call(
        forward_kernel,
        out_shape=[f32(Z_TILES, N, NY)] * 2,
        in_specs=[ANY] * 6,
        out_specs=[ANY] * 2,
        scratch_shapes=[vmem(2, X_TILES, N, NY), vmem(2, X_TILES, N, NY), vmem(2, Z_TILES, N, NY), pltpu.SemaphoreType.DMA((6,))],
        compiler_params=params(),
        name="forward",
    )(m0, m1, r0, r1, ze, zh)
    g1 = swap(q1, "grp", 1)
    g0 = swap(q0, "grp", 0)
    angles = freqs * jnp.arange(1, STEPS + 1, dtype=jnp.float32)[:, None]
    weights = jnp.stack([jnp.cos(angles), -jnp.sin(angles)], axis=2)
    fields = [vmem(3, ROWS, 2, N, NY)] * 4
    return tuple(
        pl.pallas_call(
            together_kernel,
            out_shape=[f32(3, N, N, NY), f32(3, N, N, NY), f32(2, 3, N, N, NY), f32(FREQS, 2, 3, 1, N, NY)],
            in_specs=[ANY] * 7 + [SMEM] * 5,
            out_specs=[ANY] * 4,
            scratch_shapes=fields + [vmem(2, X_TILES, N, NY), vmem(2, Z_TILES, N, NY)] + [vmem(ROWS, N, NY)] * 4 + [
                vmem(2 * STEPS, 2, N, NY), vmem(*plane), vmem(2 * STEPS, 2, N, NY), vmem(*plane),
                vmem(5, ROWS, 2, N, LANES), vmem(FREQS, 2, 3, 1, N, NY), pltpu.SemaphoreType.DMA((8,)),
            ],
            compiler_params=params(),
            name="together",
        )(e_field, h_field, polar, r0, r1, g0, g1, material, eps_table, loss_table, lorentz, weights)
    )


def solution(mesh):
    placed = (
        P(None, "grp", "dev", None),
        P(None, "grp", "dev", None),
        P(None, None, "grp", "dev", None),
        P("grp", "dev"),
        P(),
        P(),
        P(),
        P(),
    )
    return jax.shard_map(
        on_device,
        mesh=mesh,
        in_specs=placed,
        out_specs=(
            P(None, "grp", "dev", None),
            P(None, "grp", "dev", None),
            P(None, None, "grp", "dev", None),
            P(None, None, None, "grp", "dev", None),
        ),
        check_vma=False,
    )
```

```python
import jax
import jax.numpy as jnp
from jax import lax
from jax.experimental import pallas as pl
from jax.experimental.pallas import tpu as pltpu
from jax.sharding import PartitionSpec as P


STEPS = 4
FREQS = 4
COURANT = 0.5
N = 8
NY = 640
LANES = 128

ROWS = 17
Z0 = 5

X_TILES = 13
OWN_TILES = 12
FAR_TILES = 8


def ladder(first, count, start, way):
    return [(first + i, start + way * j) for i in range(count) for j in range(count - i)]


def ray_rows(entries, tile):
    out = {}
    for c in range(2):
        for kind, n, place in entries:
            k = len(out)
            out[(kind, n, c, place)] = (tile + k // 8, k % 8)
    return out


def named(kind, pairs):
    return [(kind, n, place) for n, place in pairs]


HX = ray_rows(named("ze", ladder(0, 3, 0, 1)) + named("zh", ladder(1, 3, 0, 1)), 8)
LX = ray_rows(named("ze", ladder(0, 4, 7, -1)) + named("zh", ladder(1, 3, 7, -1)), 8)
HZ = ray_rows(named("xe", ladder(0, 3, 0, 1)) + named("xh", ladder(1, 2, 0, 1)), 9)
LZ = ray_rows(named("xe", ladder(0, 3, 7, -1)) + named("xh", ladder(1, 3, 7, -1)), 9)
HF = ray_rows(named("xhl", ladder(1, 3, 0, 1)) + named("xeh", ladder(0, 3, 0, 1)), 4)
LF = ray_rows(named("xhl", ladder(1, 3, 7, -1)) + named("xeh", ladder(0, 4, 7, -1)), 3)


def ghost_place(kind, n, c, x):
    if kind == "ze":
        return {0: (c, x), 3: (c, (x + 4) % N), 1: (2 + c, x), 2: (2 + c, (x + 4) % N)}[n]
    return {1: (c, x), 3: (c, (x + 4) % N), 2: (2, (x + 4 * c) % N)}[n]


def ghost_tile(ref, kind, n, c):
    tile, row = ghost_place(kind, n, c, 0)
    value = ref[tile]
    return pltpu.roll(value, 4, 0) if row == 4 else value


def slot_e(n, c):
    return 2 * n + c


def slot_h(n, c):
    return 2 * (n - 1) + c


def wide(tile):
    return jnp.concatenate([tile] * (NY // LANES), axis=1)


def sublane(shape):
    return lax.broadcasted_iota(jnp.int32, shape, 0)


def lane(shape):
    return lax.broadcasted_iota(jnp.int32, shape, 1)


def add(x, y):
    return y if x is None else x if y is None else x + y


def sub(x, y):
    return x if y is None else -y if x is None else x - y


def mul(k, x):
    return None if x is None else k * x


def y_ahead(v):
    if v is None:
        return None
    r = pltpu.roll(v, NY - 1, 1)
    last = r[:, NY - LANES :]
    return jnp.concatenate([r[:, : NY - LANES], jnp.where(lane(last.shape) == LANES - 1, 0.0, last)], axis=1)


def y_behind(v):
    if v is None:
        return None
    r = pltpu.roll(v, 1, 1)
    first = r[:, :LANES]
    return jnp.concatenate([jnp.where(lane(first.shape) == 0, 0.0, first), r[:, LANES:]], axis=1)


def x_up(v):
    return None if v is None else pltpu.roll(v, N - 1, 0)


def x_down(v):
    return None if v is None else pltpu.roll(v, 1, 0)


def choose(edge, x, y):
    if x is None and y is None:
        return None
    return jnp.where(edge, 0.0 if x is None else x, 0.0 if y is None else y)


def kind_tables(eps_ref, loss_ref):
    out = []
    for k in range(4):
        damping = jnp.full((N, LANES), loss_ref[k], jnp.float32)
        permittivity = jnp.full((N, LANES), eps_ref[k], jnp.float32)
        scale = 1.0 / (1.0 + damping)
        inverse = 1.0 / permittivity
        out.append(((1.0 - damping) * scale, COURANT * scale, COURANT * scale * inverse, inverse))
    return out


def row_coefficients(kind, tables):
    masks = [kind == k + 1.0 for k in range(4)]
    out = []
    for j in range(4):
        total = jnp.zeros((N, LANES), jnp.float32)
        for k in range(4):
            total = jnp.where(masks[k], tables[k][j], total)
        out.append(total)
    out.append(jnp.where(masks[3], 1.0, 0.0))
    return out


def polar_scalars(lorentz_ref):
    shape = (N, LANES)
    a = jnp.full(shape, lorentz_ref[0], jnp.float32)
    g = jnp.full(shape, lorentz_ref[1], jnp.float32)
    s = jnp.full(shape, lorentz_ref[2], jnp.float32)
    scale = 1.0 / (1.0 + 0.5 * g)
    return (1.0 - a * a - 0.5 * g) * scale, (1.0 - 0.5 * g) * scale, s * a * a * scale


def own_kinds(material_ref):
    row = sublane((N, LANES))
    out = []
    for z in range(N):
        kind = jnp.zeros((N, LANES), jnp.int32)
        for x in range(N):
            kind = jnp.where(row == x, material_ref[z, x] + 1, kind)
        out.append(kind.astype(jnp.float32))
    return out


def e_update(curl, e, a, b, k, polar):
    retain, _, e_gain, inverse, active = k
    p, q, r = polar
    moved = mul(active, add(sub(mul(p, a), mul(q, b)), mul(r, e)))
    e_new = sub(add(mul(retain, e), mul(e_gain, curl)), mul(inverse, moved))
    p_new = add(a, moved)
    if b is None:
        return e_new, mul(active, p_new)
    return e_new, jnp.where(active > 0.5, p_new, b)


def start_all(pairs, sems):
    copies = [pltpu.make_async_copy(source, target, sems.at[i]) for i, (source, target) in enumerate(pairs)]
    for copy in copies:
        copy.start()
    return copies


def wait_all(copies):
    for copy in copies:
        copy.wait()


def alone_kernel(
    e_hbm, h_hbm, p_hbm, material_hbm, eps_hbm, loss_hbm, lorentz_hbm,
    m0, m1, w0, w1,
    e, h, a, b, ze, zh, xe, xh, rays, coef, material, eps, loss, lorentz, sems,
):
    high_first = lax.rem(lax.axis_index("dev"), 2) == 0
    above_first = lax.rem(lax.axis_index("grp"), 2) == 0
    small = start_all(
        [(material_hbm, material), (eps_hbm, eps), (loss_hbm, loss), (lorentz_hbm, lorentz)], sems.at[pl.ds(0, 4)]
    )
    large = start_all(
        [(e_hbm, e), (h_hbm, h), (p_hbm.at[0], a), (p_hbm.at[1], b)], sems.at[pl.ds(4, 4)]
    )
    wait_all(small)
    tables = kind_tables(eps, loss)
    polar = [wide(v) for v in polar_scalars(lorentz)]
    ln = lane((N, LANES))
    packed = jnp.zeros((N, LANES), jnp.float32)
    for z, kind in enumerate(own_kinds(material)):
        packed = jnp.where(ln == z, kind, packed)
        for j, v in enumerate(row_coefficients(kind, tables)):
            coef[j, z] = v
    packed = wide(packed)
    m0[12] = packed
    m1[12] = packed
    w0[8] = packed
    w1[8] = packed
    wait_all(large)
    row = sublane((N, NY))
    top = row == N - 1
    bottom = row == 0

    for n in range(1, STEPS + 1):
        old, new = (a, b) if n % 2 == 1 else (b, a)
        for c in range(2):
            ze[slot_e(n - 1, c)] = e[c, 0]
        for z in range(N):
            k = [wide(coef[j, z]) for j in range(5)]
            retain, h_gain = k[0], k[1]
            ex, ey, ez = (e[c, z] for c in range(3))
            e1x, e1y = (e[c, z + 1] if z < N - 1 else None for c in range(2))
            r = slot_e(n - 1, 0)
            xe[z, r : r + 1, :] = ey[0:1, :]
            xe[z, r + 1 : r + 2, :] = ez[0:1, :]
            xa_y = choose(top, None, x_up(ey))
            xa_z = choose(top, None, x_up(ez))
            hx = retain * h[0, z] - h_gain * ((y_ahead(ez) - ez) - sub(e1y, ey))
            hy = retain * h[1, z] - h_gain * (sub(e1x, ex) - (xa_z - ez))
            hz = retain * h[2, z] - h_gain * ((xa_y - ey) - (y_ahead(ex) - ex))
            h[0, z] = hx
            h[1, z] = hy
            h[2, z] = hz
            r = slot_h(n, 0)
            xh[z, r : r + 1, :] = hy[N - 1 : N, :]
            xh[z, r + 1 : r + 2, :] = hz[N - 1 : N, :]
            if n < STEPS:
                lx, ly = (h[c, z - 1] if z else None for c in range(2))
                xb_y = choose(bottom, None, x_down(hy))
                xb_z = choose(bottom, None, x_down(hz))
                curls = (
                    (hz - y_behind(hz)) - sub(hy, ly),
                    sub(hx, lx) - (hz - xb_z),
                    (hy - xb_y) - (hx - y_behind(hx)),
                )
                for c, (curl, field) in enumerate(zip(curls, (ex, ey, ez))):
                    e[c, z], new[c, z] = e_update(curl, field, old[c, z], new[c, z], k, polar)
        for c in range(2):
            zh[slot_h(n, c)] = h[c, N - 1]

    for i, table in enumerate((HX, LX)):
        for (kind, n, c, x), (tile, r) in table.items():
            source = ze.at[slot_e(n, c)] if kind == "ze" else zh.at[slot_h(n, c)]
            rays[i, tile - 8, r : r + 1, :] = source[x : x + 1, :]
    for i, table in enumerate((HZ, LZ)):
        for (kind, n, c, z), (tile, r) in table.items():
            at = slot_e(n, c) if kind == "xe" else slot_h(n, c)
            source = xe if kind == "xe" else xh
            rays[2 + i, tile - 9, r : r + 1, :] = source[z, at : at + 1, :]

    def deal(first, one, other, tile, for_above, for_below):
        one[tile] = jnp.where(first, for_above, for_below)
        other[tile] = jnp.where(first, for_below, for_above)

    for i in range(N):
        deal(high_first, m0, m1, i, xh[i], xe[i])
        deal(above_first, w0, w1, i, zh[i], ze[i])
    for i in range(4):
        deal(high_first, m0, m1, 8 + i, rays[1, i], rays[0, i])
    for i in range(3):
        deal(above_first, w0, w1, 9 + i, rays[3, i], rays[2, i])


def forward_kernel(r0, r1, v0, v1, high, low, ghosts, rays):
    high_first = lax.rem(lax.axis_index("dev"), 2) == 0
    above_first = lax.rem(lax.axis_index("grp"), 2) == 0
    for i in range(X_TILES):
        one, other = r0[i], r1[i]
        high[i] = jnp.where(high_first, one, other)
        low[i] = jnp.where(high_first, other, one)
    row = sublane((N, NY))
    packed = jnp.where(row < 3, high[12], jnp.where(row > 3, low[12], 0.0))
    rays[0, 7] = packed
    rays[1, 7] = packed
    for x, source, table in [(x, high, HX) for x in range(3)] + [(x, low, LX) for x in range(4, N)]:
        for (kind, n, c, place), (tile, r) in table.items():
            if place == x:
                to, at = ghost_place(kind, n, c, x)
                rays[0 if kind == "ze" else 1, to, at : at + 1, :] = source[tile, r : r + 1, :]
    for i, table in enumerate((HF, LF)):
        for (kind, n, c, z), (tile, r) in table.items():
            at = slot_e(n, c) if kind == "xeh" else slot_h(n, c)
            source = high if kind == "xeh" else low
            rays[i, tile, r : r + 1, :] = source[z, at : at + 1, :]
    for i in range(4):
        ghosts[i] = rays[0, i]
    for i in range(3):
        ghosts[4 + i] = rays[1, i]
    for i in range(FAR_TILES):
        below, above = rays[0, i], rays[1, i]
        v0[i] = jnp.where(above_first, above, below)
        v1[i] = jnp.where(above_first, below, above)


def plan():
    mine = {(c, z, 0) for c in range(3) for z in range(N)}
    need_h, need_e = {STEPS: set(mine)}, {STEPS: set(mine)}
    for n in range(STEPS, 0, -1):
        for c, z, s in need_e[n]:
            t = 1 - s
            need_h[n] |= {
                0: {(2, z, s), (1, z, s), (1, z - 1, s)},
                1: {(0, z, s), (0, z - 1, s), (2, z, s), (2, z, t)},
                2: {(1, z, s), (1, z, t), (0, z, s)},
            }[c]
        need_e[n - 1] = set(need_e[n])
        need_h[n - 1] = set(need_h[n])
        for c, z, s in need_h[n]:
            t = 1 - s
            need_e[n - 1] |= {
                0: {(2, z, s), (1, z, s), (1, z + 1, s)},
                1: {(0, z, s), (0, z + 1, s), (2, z, s), (2, z, t)},
                2: {(1, z, s), (1, z, t), (0, z, s)},
            }[c]
    return need_h, need_e


def together_kernel(
    e_hbm, h_hbm, p_hbm, material_hbm, eps_hbm, loss_hbm, lorentz_hbm,
    high, low, ghosts, g0, g1, f0, f1, weights,
    e_out, h_out, p_out, s_out,
    e, h, a, b, own, far, coef, seen, spectrum, material, eps, loss, lorentz, sems,
):
    above_first = lax.rem(lax.axis_index("grp"), 2) == 0
    mine = pl.ds(Z0, N)
    small = start_all(
        [(material_hbm, material), (eps_hbm, eps), (loss_hbm, loss), (lorentz_hbm, lorentz)], sems.at[pl.ds(0, 4)]
    )
    large = start_all(
        [
            (e_hbm, e.at[:, mine, 0]),
            (h_hbm, h.at[:, mine, 0]),
            (p_hbm.at[0], a.at[:, mine, 0]),
            (p_hbm.at[1], b.at[:, mine, 0]),
        ],
        sems.at[pl.ds(4, 4)],
    )
    for target, one, other, tiles in ((own, g0, g1, OWN_TILES), (far, f0, f1, FAR_TILES)):
        for i in range(tiles):
            x, y = one[i], other[i]
            target[0, i] = jnp.where(above_first, x, y)
            target[1, i] = jnp.where(above_first, y, x)
    above, below = own.at[0], own.at[1]
    far_above, far_below = far.at[0], far.at[1]
    wait_all(small)
    tables = kind_tables(eps, loss)
    polar = [wide(v) for v in polar_scalars(lorentz)]
    narrow = sublane((N, LANES))
    kinds = {(z, 0): kind for z, kind in enumerate(own_kinds(material))}
    side = jnp.where(narrow < 3, high[12, :, 0:LANES], jnp.where(narrow > 3, low[12, :, 0:LANES], 0.0))
    columns = [(z, 1, side, z) for z in range(N)]
    for z in (*range(-4, 0), *range(N, N + 3)):
        near, corner = (below, far_below) if z < 0 else (above, far_above)
        columns += [(z, 0, near[8, :, 0:LANES], z % N), (z, 1, corner[7, :, 0:LANES], z % N)]
    for z, s, tile, at in columns:
        kinds[(z, s)] = jnp.broadcast_to(tile[:, at : at + 1], (N, LANES))
    for (z, s), kind in kinds.items():
        for j, v in enumerate(row_coefficients(kind, tables)):
            coef[j, Z0 + z, s] = v
    wait_all(large)

    row = sublane((N, NY))
    top = row == N - 1
    bottom = row == 0

    def lookup(table, near, far_table, far_near, kind, n, c, z):
        for t, ref in ((table, near), (far_table, far_near)):
            if (kind, n, c, z) in t:
                tile, r = t[(kind, n, c, z)]
                return ref[tile, r : r + 1, :]
        return None

    def x_source(kind, n, c, z):
        if 0 <= z < N:
            if kind in ("xe", "xh"):
                return None
            r = slot_e(n, c) if kind == "xeh" else slot_h(n, c)
            return (high if kind == "xeh" else low)[z, r : r + 1, :]
        if z >= N:
            found = lookup(HZ, above, HF, far_above, kind, n, c, z - N)
        else:
            found = lookup(LZ, below, LF, far_below, kind, n, c, z + N)
        return found

    def z_source(kind, n, c, z, s):
        if kind == "ze" and z == N:
            return above[slot_e(n, c)] if s == 0 else ghost_tile(far_above, "ze", n, c)
        if kind == "ze" and z == 0 and s == 1 and n < 3:
            return ghost_tile(ghosts, "ze", n, c)
        if kind == "zh" and z == -1:
            if s == 0:
                return below[slot_h(n, c)]
            return ghost_tile(far_below, "zh", n, c) if n < 4 else None
        if kind == "zh" and z == N - 1 and s == 1 and n < 4:
            return ghost_tile(ghosts.at[pl.ds(4, 3)], "zh", n, c)
        return None

    def across(v, shift, edge, s0, s1):
        v0, v1 = shift(v[0]), shift(v[1])
        return choose(edge, add(v1, s0), v0), choose(edge, add(v0, s1), v1)

    need_h, need_e = plan()
    live = {(f, c, z, 0) for f in range(4) for c in range(3) for z in range(N)}

    def get(f, c, z, s):
        return (e, h, a, b)[f][c, Z0 + z, s] if (f, c, z, s) in live else None

    def put(f, c, z, s, value):
        if value is not None:
            (e, h, a, b)[f][c, Z0 + z, s] = value
            live.add((f, c, z, s))

    outs = []
    for n in range(1, STEPS + 1):
        old, new = (2, 3) if n % 2 == 1 else (3, 2)
        for z in range(-4, N + 3):
            todo = {(c, s) for c, at, s in need_h[n] if at == z}
            ey = [get(0, 1, z, s) for s in range(2)]
            ez = [get(0, 2, z, s) for s in range(2)]
            xa_y = xa_z = (None, None)
            if todo:
                xa_y = across(ey, x_up, top, x_source("xeh", n - 1, 0, z), x_source("xe", n - 1, 0, z))
                xa_z = across(ez, x_up, top, x_source("xeh", n - 1, 1, z), x_source("xe", n - 1, 1, z))
            for s in range(2):
                if not any((c, s) in todo for c in range(3)):
                    continue
                k = [wide(coef[j, Z0 + z, s]) for j in range(2)]
                ex = get(0, 0, z, s)
                e1x = add(get(0, 0, z + 1, s), z_source("ze", n - 1, 0, z + 1, s))
                e1y = add(get(0, 1, z + 1, s), z_source("ze", n - 1, 1, z + 1, s))
                curls = (
                    lambda: sub(sub(y_ahead(ez[s]), ez[s]), sub(e1y, ey[s])),
                    lambda: sub(sub(e1x, ex), sub(xa_z[s], ez[s])),
                    lambda: sub(sub(xa_y[s], ey[s]), sub(y_ahead(ex), ex)),
                )
                for c in range(3):
                    if (c, s) in todo:
                        put(1, c, z, s, sub(mul(k[0], get(1, c, z, s)), mul(k[1], curls[c]())))
            todo = {(c, s) for c, at, s in need_e[n] if at == z}
            if not todo:
                continue
            hy = [get(1, 1, z, s) for s in range(2)]
            hz = [get(1, 2, z, s) for s in range(2)]
            xb_y = across(hy, x_down, bottom, x_source("xhl", n, 0, z), x_source("xh", n, 0, z))
            xb_z = across(hz, x_down, bottom, x_source("xhl", n, 1, z), x_source("xh", n, 1, z))
            for s in range(2):
                if not any((c, s) in todo for c in range(3)):
                    continue
                k = [wide(coef[j, Z0 + z, s]) for j in range(5)]
                hx = get(1, 0, z, s)
                lx = add(get(1, 0, z - 1, s), z_source("zh", n, 0, z - 1, s))
                ly = add(get(1, 1, z - 1, s), z_source("zh", n, 1, z - 1, s))
                curls = (
                    lambda: sub(sub(hz[s], y_behind(hz[s])), sub(hy[s], ly)),
                    lambda: sub(sub(hx, lx), sub(hz[s], xb_z[s])),
                    lambda: sub(sub(hy[s], xb_y[s]), sub(hx, y_behind(hx))),
                )
                for c in range(3):
                    if (c, s) in todo:
                        e_new, p_new = e_update(
                            curls[c](), get(0, c, z, s), get(old, c, z, s), get(new, c, z, s), k, polar
                        )
                        put(0, c, z, s, e_new)
                        if n < STEPS or s == 0:
                            put(new, c, z, s, p_new)
            if z == N // 2:
                for c in range(3):
                    seen[n - 1, c] = e[c, Z0 + z, 0]
            if n == STEPS:
                at = Z0 + z
                outs += start_all(
                    [
                        (e.at[:, at, 0], e_out.at[:, z]),
                        (h.at[:, at, 0], h_out.at[:, z]),
                        (a.at[:, at, 0], p_out.at[0, :, z]),
                        (b.at[:, at, 0], p_out.at[1, :, z]),
                    ],
                    sems.at[pl.ds(8 + 4 * z, 4)],
                )
                if z == N // 2:
                    for c in range(3):
                        planes = [seen[i, c] for i in range(STEPS)]
                        for f in range(FREQS):
                            for q in range(2):
                                total = weights[0, f, q] * planes[0]
                                for i in range(1, STEPS):
                                    total = total + weights[i, f, q] * planes[i]
                                spectrum[f, q, c, 0] = total
                    outs += start_all([(spectrum, s_out)], sems.at[pl.ds(40, 1)])
    wait_all(outs)


HBM = pl.BlockSpec(memory_space=pltpu.HBM)
VMEM = pl.BlockSpec(memory_space=pltpu.VMEM)
SMEM = pl.BlockSpec(memory_space=pltpu.SMEM)


def f32(*shape):
    return jax.ShapeDtypeStruct(shape, jnp.float32)


def vmem(*shape):
    return pltpu.VMEM(shape, jnp.float32)


def small_tables():
    return [pltpu.SMEM((N, N), jnp.int32), pltpu.SMEM((4,), jnp.float32), pltpu.SMEM((4,), jnp.float32), pltpu.SMEM((3,), jnp.float32)]


def params():
    return pltpu.CompilerParams(vmem_limit_bytes=32 * 1024 * 1024)


def swap(block, axis, parity):
    size = lax.axis_size(axis)
    route = []
    for i in range(parity, size - 1, 2):
        route += [(i, i + 1), (i + 1, i)]
    return lax.ppermute(block, axis, route)


def call_alone(inputs):
    plane = (2 * STEPS, N, NY)
    return pl.pallas_call(
        alone_kernel,
        out_shape=[f32(X_TILES, N, NY)] * 2 + [f32(OWN_TILES, N, NY)] * 2,
        in_specs=[HBM] * 7,
        out_specs=[VMEM] * 4,
        scratch_shapes=[vmem(3, N, N, NY)] * 4
        + [vmem(*plane)] * 4
        + [vmem(4, 4, N, NY), vmem(5, N, N, LANES)]
        + small_tables()
        + [pltpu.SemaphoreType.DMA((8,))],
        compiler_params=params(),
        name="alone",
    )(*inputs)


def call_forward(r0, r1):
    return pl.pallas_call(
        forward_kernel,
        out_shape=[f32(FAR_TILES, N, NY)] * 2 + [f32(X_TILES, N, NY)] * 2 + [f32(7, N, NY)],
        in_specs=[VMEM] * 2,
        out_specs=[VMEM] * 5,
        scratch_shapes=[vmem(2, FAR_TILES, N, NY)],
        compiler_params=params(),
        name="forward",
    )(r0, r1)


def call_together(inputs, received, weights):
    return pl.pallas_call(
        together_kernel,
        out_shape=[f32(3, N, N, NY), f32(3, N, N, NY), f32(2, 3, N, N, NY), f32(FREQS, 2, 3, 1, N, NY)],
        in_specs=[HBM] * 7 + [VMEM] * 7 + [SMEM],
        out_specs=[HBM] * 4,
        scratch_shapes=[vmem(3, ROWS, 2, N, NY)] * 4
        + [
            vmem(2, OWN_TILES, N, NY),
            vmem(2, FAR_TILES, N, NY),
            vmem(5, ROWS, 2, N, LANES),
            vmem(STEPS, 3, N, NY),
            vmem(FREQS, 2, 3, 1, N, NY),
        ]
        + small_tables()
        + [pltpu.SemaphoreType.DMA((41,))],
        compiler_params=params(),
        name="together",
    )(*inputs, *received, weights)


def on_device(e_field, h_field, polar, material, eps_table, loss_table, lorentz, freqs):
    inputs = (e_field, h_field, polar, material, eps_table, loss_table, lorentz)
    m0, m1, w0, w1 = call_alone(inputs)
    r1 = swap(m1, "dev", 1)
    r0 = swap(m0, "dev", 0)
    g1 = swap(w1, "grp", 1)
    g0 = swap(w0, "grp", 0)
    v0, v1, high, low, ghosts = call_forward(r0, r1)
    f1 = swap(v1, "grp", 1)
    f0 = swap(v0, "grp", 0)
    angles = freqs * jnp.arange(1, STEPS + 1, dtype=jnp.float32)[:, None]
    weights = jnp.stack([jnp.cos(angles), -jnp.sin(angles)], axis=2)
    return tuple(call_together(inputs, (high, low, ghosts, g0, g1, f0, f1), weights))


def solution(mesh):
    placed = (
        P(None, "grp", "dev", None),
        P(None, "grp", "dev", None),
        P(None, None, "grp", "dev", None),
        P("grp", "dev"),
        P(),
        P(),
        P(),
        P(),
    )
    return jax.shard_map(
        on_device,
        mesh=mesh,
        in_specs=placed,
        out_specs=(
            P(None, "grp", "dev", None),
            P(None, "grp", "dev", None),
            P(None, None, "grp", "dev", None),
            P(None, None, None, "grp", "dev", None),
        ),
        check_vma=False,
    )
```

```python
import functools

import jax
import jax.numpy as jnp
from jax import lax
from jax.experimental import pallas as pl
from jax.experimental.pallas import tpu as pltpu
from jax.sharding import PartitionSpec as P


STEPS = 4
FREQS = 4
COURANT = 0.5
N = 8
NY = 640
LANES = 128

ROWS = 17
Z0 = 5

X_TILES = 13
OWN_TILES = 12
FAR_TILES = 8


def ladder(first, count, start, way):
    return [(first + i, start + way * j) for i in range(count) for j in range(count - i)]


def ray_rows(entries, tile):
    out = {}
    for c in range(2):
        for kind, n, place in entries:
            k = len(out)
            out[(kind, n, c, place)] = (tile + k // 8, k % 8)
    return out


def named(kind, pairs):
    return [(kind, n, place) for n, place in pairs]


HX = ray_rows(named("ze", ladder(0, 3, 0, 1)) + named("zh", ladder(1, 3, 0, 1)), 8)
LX = ray_rows(named("ze", ladder(0, 4, 7, -1)) + named("zh", ladder(1, 3, 7, -1)), 8)
HZ = ray_rows(named("xe", ladder(0, 3, 0, 1)) + named("xh", ladder(1, 2, 0, 1)), 9)
LZ = ray_rows(named("xe", ladder(0, 3, 7, -1)) + named("xh", ladder(1, 3, 7, -1)), 9)
HF = ray_rows(named("xhl", ladder(1, 3, 0, 1)) + named("xeh", ladder(0, 3, 0, 1)), 4)
LF = ray_rows(named("xhl", ladder(1, 3, 7, -1)) + named("xeh", ladder(0, 4, 7, -1)), 3)


def ghost_place(kind, n, c, x):
    if kind == "ze":
        return {0: (c, x), 3: (c, (x + 4) % N), 1: (2 + c, x), 2: (2 + c, (x + 4) % N)}[n]
    return {1: (c, x), 3: (c, (x + 4) % N), 2: (2, (x + 4 * c) % N)}[n]


def ghost_tile(ref, kind, n, c):
    tile, row = ghost_place(kind, n, c, 0)
    value = ref[tile]
    return pltpu.roll(value, 4, 0) if row == 4 else value


def slot_e(n, c):
    return 2 * n + c


def slot_h(n, c):
    return 2 * (n - 1) + c


def wide(tile):
    return jnp.concatenate([tile] * (NY // LANES), axis=1)


def sublane(shape):
    return lax.broadcasted_iota(jnp.int32, shape, 0)


def lane(shape):
    return lax.broadcasted_iota(jnp.int32, shape, 1)


def add(x, y):
    return y if x is None else x if y is None else x + y


def sub(x, y):
    return x if y is None else -y if x is None else x - y


def mul(k, x):
    return None if x is None else k * x


def y_ahead(v):
    if v is None:
        return None
    r = pltpu.roll(v, NY - 1, 1)
    last = r[:, NY - LANES :]
    return jnp.concatenate([r[:, : NY - LANES], jnp.where(lane(last.shape) == LANES - 1, 0.0, last)], axis=1)


def y_behind(v):
    if v is None:
        return None
    r = pltpu.roll(v, 1, 1)
    first = r[:, :LANES]
    return jnp.concatenate([jnp.where(lane(first.shape) == 0, 0.0, first), r[:, LANES:]], axis=1)


def x_up(v):
    return None if v is None else pltpu.roll(v, N - 1, 0)


def x_down(v):
    return None if v is None else pltpu.roll(v, 1, 0)


def choose(edge, x, y):
    if x is None and y is None:
        return None
    return jnp.where(edge, 0.0 if x is None else x, 0.0 if y is None else y)


def kind_tables(eps_ref, loss_ref):
    out = []
    for k in range(4):
        damping = jnp.full((N, LANES), loss_ref[k], jnp.float32)
        permittivity = jnp.full((N, LANES), eps_ref[k], jnp.float32)
        scale = 1.0 / (1.0 + damping)
        inverse = 1.0 / permittivity
        out.append(((1.0 - damping) * scale, COURANT * scale, COURANT * scale * inverse, inverse))
    return out


def row_coefficients(kind, tables):
    masks = [kind == k + 1.0 for k in range(4)]
    out = []
    for j in range(4):
        total = jnp.zeros((N, LANES), jnp.float32)
        for k in range(4):
            total = jnp.where(masks[k], tables[k][j], total)
        out.append(total)
    out.append(jnp.where(masks[3], 1.0, 0.0))
    return out


def polar_scalars(lorentz_ref):
    shape = (N, LANES)
    a = jnp.full(shape, lorentz_ref[0], jnp.float32)
    g = jnp.full(shape, lorentz_ref[1], jnp.float32)
    s = jnp.full(shape, lorentz_ref[2], jnp.float32)
    scale = 1.0 / (1.0 + 0.5 * g)
    return (1.0 - a * a - 0.5 * g) * scale, (1.0 - 0.5 * g) * scale, s * a * a * scale


def own_kinds(material_ref):
    row = sublane((N, LANES))
    out = []
    for z in range(N):
        kind = jnp.zeros((N, LANES), jnp.int32)
        for x in range(N):
            kind = jnp.where(row == x, material_ref[z, x] + 1, kind)
        out.append(kind.astype(jnp.float32))
    return out


def e_update(curl, e, a, b, k, polar):
    retain, _, e_gain, inverse, active = k
    p, q, r = polar
    moved = mul(active, add(sub(mul(p, a), mul(q, b)), mul(r, e)))
    e_new = sub(add(mul(retain, e), mul(e_gain, curl)), mul(inverse, moved))
    p_new = add(a, moved)
    if b is None:
        return e_new, mul(active, p_new)
    return e_new, jnp.where(active > 0.5, p_new, b)


def start_all(pairs, sems):
    copies = [pltpu.make_async_copy(source, target, sems.at[i]) for i, (source, target) in enumerate(pairs)]
    for copy in copies:
        copy.start()
    return copies


def wait_all(copies):
    for copy in copies:
        copy.wait()


def alone_kernel(
    e_hbm, h_hbm, p_hbm, material_hbm, eps_hbm, loss_hbm, lorentz_hbm,
    m0, m1, w0, w1, coef, shared,
    e, h, a, b, ze, zh, xe, xh, rays, material, eps, loss, lorentz, sems,
):
    high_first = lax.rem(lax.axis_index("dev"), 2) == 0
    above_first = lax.rem(lax.axis_index("grp"), 2) == 0
    small = start_all(
        [(material_hbm, material), (eps_hbm, eps), (loss_hbm, loss), (lorentz_hbm, lorentz)], sems.at[pl.ds(0, 4)]
    )
    large = start_all(
        [(e_hbm, e), (h_hbm, h), (p_hbm.at[0], a), (p_hbm.at[1], b)], sems.at[pl.ds(4, 4)]
    )
    wait_all(small)
    tables = kind_tables(eps, loss)
    polar = polar_scalars(lorentz)
    for i, v in enumerate([v for table in tables for v in table] + list(polar)):
        shared[i] = v
    polar = [wide(v) for v in polar]
    ln = lane((N, LANES))
    packed = jnp.zeros((N, LANES), jnp.float32)
    for z, kind in enumerate(own_kinds(material)):
        packed = jnp.where(ln == z, kind, packed)
        for j, v in enumerate(row_coefficients(kind, tables)):
            coef[j, z] = v
    packed = wide(packed)
    m0[12] = packed
    m1[12] = packed
    w0[8] = packed
    w1[8] = packed
    wait_all(large)
    row = sublane((N, NY))
    top = row == N - 1
    bottom = row == 0

    for n in range(1, STEPS + 1):
        old, new = (a, b) if n % 2 == 1 else (b, a)
        for c in range(2):
            ze[slot_e(n - 1, c)] = e[c, 0]
        for z in range(N):
            k = [wide(coef[j, z]) for j in range(5)]
            retain, h_gain = k[0], k[1]
            ex, ey, ez = (e[c, z] for c in range(3))
            e1x, e1y = (e[c, z + 1] if z < N - 1 else None for c in range(2))
            r = slot_e(n - 1, 0)
            xe[z, r : r + 1, :] = ey[0:1, :]
            xe[z, r + 1 : r + 2, :] = ez[0:1, :]
            xa_y = choose(top, None, x_up(ey))
            xa_z = choose(top, None, x_up(ez))
            hx = retain * h[0, z] - h_gain * ((y_ahead(ez) - ez) - sub(e1y, ey))
            hy = retain * h[1, z] - h_gain * (sub(e1x, ex) - (xa_z - ez))
            hz = retain * h[2, z] - h_gain * ((xa_y - ey) - (y_ahead(ex) - ex))
            h[0, z] = hx
            h[1, z] = hy
            h[2, z] = hz
            r = slot_h(n, 0)
            xh[z, r : r + 1, :] = hy[N - 1 : N, :]
            xh[z, r + 1 : r + 2, :] = hz[N - 1 : N, :]
            if n < STEPS:
                lx, ly = (h[c, z - 1] if z else None for c in range(2))
                xb_y = choose(bottom, None, x_down(hy))
                xb_z = choose(bottom, None, x_down(hz))
                curls = (
                    (hz - y_behind(hz)) - sub(hy, ly),
                    sub(hx, lx) - (hz - xb_z),
                    (hy - xb_y) - (hx - y_behind(hx)),
                )
                for c, (curl, field) in enumerate(zip(curls, (ex, ey, ez))):
                    e[c, z], new[c, z] = e_update(curl, field, old[c, z], new[c, z], k, polar)
        for c in range(2):
            zh[slot_h(n, c)] = h[c, N - 1]

    for i, table in enumerate((HX, LX)):
        for (kind, n, c, x), (tile, r) in table.items():
            source = ze.at[slot_e(n, c)] if kind == "ze" else zh.at[slot_h(n, c)]
            rays[i, tile - 8, r : r + 1, :] = source[x : x + 1, :]
    for i, table in enumerate((HZ, LZ)):
        for (kind, n, c, z), (tile, r) in table.items():
            at = slot_e(n, c) if kind == "xe" else slot_h(n, c)
            source = xe if kind == "xe" else xh
            rays[2 + i, tile - 9, r : r + 1, :] = source[z, at : at + 1, :]

    def deal(first, one, other, tile, for_above, for_below):
        one[tile] = jnp.where(first, for_above, for_below)
        other[tile] = jnp.where(first, for_below, for_above)

    for i in range(N):
        deal(high_first, m0, m1, i, xh[i], xe[i])
        deal(above_first, w0, w1, i, zh[i], ze[i])
    for i in range(4):
        deal(high_first, m0, m1, 8 + i, rays[1, i], rays[0, i])
    for i in range(3):
        deal(above_first, w0, w1, 9 + i, rays[3, i], rays[2, i])


def forward_kernel(r1, r0, v1, v0, high, low, ghosts, rays):
    high_first = lax.rem(lax.axis_index("dev"), 2) == 0
    above_first = lax.rem(lax.axis_index("grp"), 2) == 0
    for i in range(X_TILES):
        one, other = r0[i], r1[i]
        high[i] = jnp.where(high_first, one, other)
        low[i] = jnp.where(high_first, other, one)
    row = sublane((N, NY))
    packed = jnp.where(row < 3, high[12], jnp.where(row > 3, low[12], 0.0))
    rays[0, 7] = packed
    rays[1, 7] = packed
    for x, source, table in [(x, high, HX) for x in range(3)] + [(x, low, LX) for x in range(4, N)]:
        for (kind, n, c, place), (tile, r) in table.items():
            if place == x:
                to, at = ghost_place(kind, n, c, x)
                rays[0 if kind == "ze" else 1, to, at : at + 1, :] = source[tile, r : r + 1, :]
    for i, table in enumerate((HF, LF)):
        for (kind, n, c, z), (tile, r) in table.items():
            at = slot_e(n, c) if kind == "xeh" else slot_h(n, c)
            source = high if kind == "xeh" else low
            rays[i, tile, r : r + 1, :] = source[z, at : at + 1, :]
    for i in range(4):
        ghosts[i] = rays[0, i]
    for i in range(3):
        ghosts[4 + i] = rays[1, i]
    for i in range(FAR_TILES):
        below, above = rays[0, i], rays[1, i]
        v0[i] = jnp.where(above_first, above, below)
        v1[i] = jnp.where(above_first, below, above)


def h_inputs(c, z, s):
    if c == 0:
        return [(2, z, s), (1, z, s), (1, z + 1, s)], [("z", 1)]
    if c == 1:
        return [(0, z, s), (0, z + 1, s), (2, z, s), (2, z, 1 - s)], [("z", 0), ("x", 1)]
    return [(1, z, s), (1, z, 1 - s), (0, z, s)], [("x", 0)]


def e_inputs(c, z, s):
    if c == 0:
        return [(2, z, s), (1, z, s), (1, z - 1, s)], [("z", 1)]
    if c == 1:
        return [(0, z, s), (0, z - 1, s), (2, z, s), (2, z, 1 - s)], [("z", 0), ("x", 1)]
    return [(1, z, s), (1, z, 1 - s), (0, z, s)], [("x", 0)]


def x_source(kind, n, c, z):
    if 0 <= z < N:
        r = slot_e(n, c) if kind == "xeh" else slot_h(n, c)
        return {"xeh": ("high", z, r), "xhl": ("low", z, r)}.get(kind)
    near, far, place = (HZ, HF, z - N) if z >= N else (LZ, LF, z + N)
    for name, table in (("own", near), ("far", far)):
        if (kind, n, c, place) in table:
            return (name, 0 if z >= N else 1, *table[(kind, n, c, place)])
    return None


def z_source(kind, n, c, z, s):
    if kind == "ze" and z == N:
        return ("own", 0, slot_e(n, c)) if s == 0 else ("far", 0, kind, n, c)
    if kind == "ze" and z == 0 and s == 1 and n < STEPS - 1:
        return ("ghosts", kind, n, c)
    if kind == "zh" and z == -1 and (s == 0 or n < STEPS):
        return ("own", 1, slot_h(n, c)) if s == 0 else ("far", 1, kind, n, c)
    if kind == "zh" and z == N - 1 and s == 1 and n < STEPS:
        return ("ghosts", kind, n, c)
    return None


def sources(field, n, z, s, wanted):
    out = []
    for border, c in wanted:
        if field == "h":
            at = x_source("xe" if s else "xeh", n - 1, c, z) if border == "x" else z_source("ze", n - 1, c, z + 1, s)
        else:
            at = x_source("xh" if s else "xhl", n, c, z) if border == "x" else z_source("zh", n, c, z - 1, s)
        out.append(at)
    return [at for at in out if at is not None]


def plan():
    mine = {(c, z, 0) for c in range(3) for z in range(N)}
    need = {("h", STEPS): set(mine), ("e", STEPS): set(mine)}
    for n in range(STEPS, 0, -1):
        for key in need[("e", n)]:
            need[("h", n)] |= set(e_inputs(*key)[0])
        need[("e", n - 1)] = set(need[("e", n)])
        need[("h", n - 1)] = set(need[("h", n)])
        for key in need[("h", n)]:
            need[("e", n - 1)] |= set(h_inputs(*key)[0])
    late = {("e", 0): set(), ("h", 0): set()}
    for n in range(1, STEPS + 1):
        for field, other, inputs, back in (("h", "e", h_inputs, n - 1), ("e", "h", e_inputs, n)):
            late[(field, n)] = set()
            for key in need[(field, n)]:
                before, wanted = inputs(*key)
                c, z, s = key
                if (
                    (s == 1 and not 0 <= z < N)
                    or key in late[(field, n - 1)]
                    or any(k in late[(other, back)] for k in before)
                    or any(at[0] == "far" for at in sources(field, n, z, s, wanted))
                ):
                    late[(field, n)].add(key)
    return need, late


NEED, LATE = plan()
FIELDS = {"e": 0, "h": 1, 0: 2, 1: 3}


class Pass:
    def __init__(self, second, live, stores, coefs, polar, places, row):
        self.second, self.live, self.stores = second, live, stores
        self.coefs, self.polar, self.places = coefs, polar, places
        self.top, self.bottom = row == N - 1, row == 0
        self.memo = {}

    def once(self, key, make):
        if key not in self.memo:
            self.memo[key] = make()
        return self.memo[key]

    def store(self, field, c, z, s, n):
        late = n > 0 and (c, z, s) in LATE[("h" if field == "h" else "e", n)]
        return self.stores[late][FIELDS[field]]

    def get(self, field, c, z, s, n):
        key = (field, c, z, s)
        if self.live.get(key, STEPS + 1) > n:
            return None
        made = n if field in ("e", "h") else n - 1 if (n - 1) % 2 == field else n - 2
        return self.once((*key, n), lambda: self.store(field, c, z, s, made)[c, Z0 + z, s])

    def put(self, field, c, z, s, n, value):
        if value is None:
            return
        self.store(field, c, z, s, n)[c, Z0 + z, s] = value
        self.live.setdefault((field, c, z, s), n)
        self.memo[(field, c, z, s, n)] = value

    def source(self, at):
        if at is None:
            return None
        if at[0] == "ghosts" or len(at) == 5:
            ref = self.places[at[0]] if at[0] == "ghosts" else self.places["far"].at[at[1]]
            kind, n, c = at[-3:]
            if at[0] == "ghosts" and kind == "zh":
                ref = ref.at[pl.ds(4, 3)]
            return ghost_tile(ref, kind, n, c)
        ref = self.places[at[0]]
        if at[0] in ("high", "low"):
            return ref[at[1], at[2] : at[2] + 1, :]
        if len(at) == 3:
            return ref[at[1], at[2]]
        return ref[at[1], at[2], at[3] : at[3] + 1, :]

    def k(self, j, z, s):
        coef = self.coefs[s == 1 and not 0 <= z < N]
        return self.once(("k", j, z, s), lambda: wide(coef[j, Z0 + z, s]))

    def x_neighbour(self, field, c, z, s, n):
        shift, edge = (x_up, self.top) if field == "e" else (x_down, self.bottom)

        def moved(half):
            return self.once(("x", field, c, z, half, n), lambda: shift(self.get(field, c, z, half, n)))

        kinds = ("xeh", "xe") if field == "e" else ("xhl", "xh")
        from_block = self.source(x_source(kinds[s], n, c - 1, z))
        return choose(edge, add(moved(1 - s), from_block), moved(s))

    def y_neighbour(self, field, c, z, s, n):
        shift = y_ahead if field == "e" else y_behind
        return self.once(("y", field, c, z, s, n), lambda: shift(self.get(field, c, z, s, n)))

    def z_neighbour(self, field, c, z, s, n):
        kind, at = ("ze", z + 1) if field == "e" else ("zh", z - 1)
        return add(self.get(field, c, at, s, n), self.source(z_source(kind, n, c, at, s)))

    def step_h(self, n, c, z, s):
        m = n - 1
        ex, ey, ez = (lambda c=c: self.get("e", c, z, s, m) for c in range(3))
        if c == 0:
            curl = sub(sub(self.y_neighbour("e", 2, z, s, m), ez()), sub(self.z_neighbour("e", 1, z, s, m), ey()))
        elif c == 1:
            curl = sub(sub(self.z_neighbour("e", 0, z, s, m), ex()), sub(self.x_neighbour("e", 2, z, s, m), ez()))
        else:
            curl = sub(sub(self.x_neighbour("e", 1, z, s, m), ey()), sub(self.y_neighbour("e", 0, z, s, m), ex()))
        value = sub(mul(self.k(0, z, s), self.get("h", c, z, s, m)), mul(self.k(1, z, s), curl))
        self.put("h", c, z, s, n, value)

    def step_e(self, n, c, z, s):
        hx, hy, hz = (lambda c=c: self.get("h", c, z, s, n) for c in range(3))
        if c == 0:
            curl = sub(sub(hz(), self.y_neighbour("h", 2, z, s, n)), sub(hy(), self.z_neighbour("h", 1, z, s, n)))
        elif c == 1:
            curl = sub(sub(hx(), self.z_neighbour("h", 0, z, s, n)), sub(hz(), self.x_neighbour("h", 2, z, s, n)))
        else:
            curl = sub(sub(hy(), self.x_neighbour("h", 1, z, s, n)), sub(hx(), self.y_neighbour("h", 0, z, s, n)))
        old, new = (n - 1) % 2, n % 2
        k = [self.k(j, z, s) for j in range(5)]
        e_new, p_new = e_update(
            curl, self.get("e", c, z, s, n - 1), self.get(old, c, z, s, n), self.get(new, c, z, s, n), k, self.polar
        )
        self.put("e", c, z, s, n, e_new)
        if n < STEPS or s == 0:
            self.put(new, c, z, s, n, p_new)

    def row(self, n, z, seen):
        for field, step in (("h", self.step_h), ("e", self.step_e)):
            for s in range(2):
                for c in range(3):
                    if (c, z, s) in NEED[(field, n)] and ((c, z, s) in LATE[(field, n)]) == self.second:
                        step(n, c, z, s)
                        if field == "e" and (c, z, s) == (c, N // 2, 0):
                            seen[n - 1, c] = self.get("e", c, z, s, n)
        self.memo = {}


def near_kernel(
    live, e_hbm, h_hbm, p_hbm, coef_in, tables, high, low, ghosts, g1, g0,
    e, h, a, b, coef, own, seen,
    sems,
):
    above_first = lax.rem(lax.axis_index("grp"), 2) == 0
    mine = pl.ds(Z0, N)
    large = start_all(
        [
            (e_hbm, e.at[:, mine, 0]),
            (h_hbm, h.at[:, mine, 0]),
            (p_hbm.at[0], a.at[:, mine, 0]),
            (p_hbm.at[1], b.at[:, mine, 0]),
        ],
        sems,
    )
    for i in range(OWN_TILES):
        x, y = g0[i], g1[i]
        own[0, i] = jnp.where(above_first, x, y)
        own[1, i] = jnp.where(above_first, y, x)
    narrow = sublane((N, LANES))
    side = jnp.where(narrow < 3, high[12, :, 0:LANES], jnp.where(narrow > 3, low[12, :, 0:LANES], 0.0))
    columns = [(z, 1, side, z) for z in range(N)]
    columns += [(z, 0, own[1 if z < 0 else 0, 8, :, 0:LANES], z % N) for z in (*range(-4, 0), *range(N, N + 3))]
    fill_coefficients(coef, columns, tables)
    for z in range(N):
        for j in range(5):
            coef[j, Z0 + z, 0] = coef_in[j, z]
    polar = [wide(tables[16 + j]) for j in range(3)]
    wait_all(large)
    live.update({(field, c, z, 0): 0 for field in FIELDS for c in range(3) for z in range(N)})
    places = {"own": own, "high": high, "low": low, "ghosts": ghosts}
    run = Pass(False, live, [(e, h, a, b)] * 2, [coef, None], polar, places, sublane((N, NY)))
    for n in range(1, STEPS + 1):
        for z in range(-4, N + 3):
            run.row(n, z, seen)


def fill_coefficients(coef, columns, tables):
    stacked = [[tables[4 * k + j] for j in range(4)] for k in range(4)]
    for z, s, tile, at in columns:
        kind = jnp.broadcast_to(tile[:, at : at + 1], (N, LANES))
        for j, v in enumerate(row_coefficients(kind, stacked)):
            coef[j, Z0 + z, s] = v


def far_kernel(
    live, e_in, h_in, a_in, b_in, coef_in, own, seen_in, tables, high, low, ghosts, f1, f0, weights,
    e_out, h_out, p_out, s_out,
    e, h, a, b, coef, seen, far, spectrum, sems,
):
    above_first = lax.rem(lax.axis_index("grp"), 2) == 0
    for i in range(FAR_TILES):
        x, y = f0[i], f1[i]
        far[0, i] = jnp.where(above_first, x, y)
        far[1, i] = jnp.where(above_first, y, x)
    columns = [(z, 1, far[1 if z < 0 else 0, 7, :, 0:LANES], z % N) for z in (*range(-4, 0), *range(N, N + 3))]
    fill_coefficients(coef, columns, tables)
    polar = [wide(tables[16 + j]) for j in range(3)]
    places = {"own": own, "far": far, "high": high, "low": low, "ghosts": ghosts}
    run = Pass(True, live, [(e_in, h_in, a_in, b_in), (e, h, a, b)], [coef_in, coef], polar, places, sublane((N, NY)))
    for field, n, last, made in ((0, STEPS, a, a_in), (1, STEPS - 1, b, b_in), ("e", STEPS, e, e_in), ("h", STEPS, h, h_in)):
        for c in range(3):
            for z in range(N):
                if (c, z, 0) not in LATE[("h" if field == "h" else "e", n)]:
                    last[c, Z0 + z, 0] = made[c, Z0 + z, 0]
    outs = []
    for n in range(1, STEPS + 1):
        for z in range(-4, N + 3):
            run.row(n, z, seen)
            if n == STEPS and 0 <= z < N:
                at = Z0 + z
                outs += start_all(
                    [
                        (e.at[:, at, 0], e_out.at[:, z]),
                        (h.at[:, at, 0], h_out.at[:, z]),
                        (a.at[:, at, 0], p_out.at[0, :, z]),
                        (b.at[:, at, 0], p_out.at[1, :, z]),
                    ],
                    sems.at[pl.ds(4 * z, 4)],
                )
                if z == N // 2:
                    for c in range(3):
                        planes = [
                            (seen if (c, z, 0) in LATE[("e", i + 1)] else seen_in)[i, c] for i in range(STEPS)
                        ]
                        for f in range(FREQS):
                            for q in range(2):
                                total = weights[0, f, q] * planes[0]
                                for i in range(1, STEPS):
                                    total = total + weights[i, f, q] * planes[i]
                                spectrum[f, q, c, 0] = total
                    outs += start_all([(spectrum, s_out)], sems.at[pl.ds(4 * N, 1)])
    wait_all(outs)


HBM = pl.BlockSpec(memory_space=pltpu.HBM)
VMEM = pl.BlockSpec(memory_space=pltpu.VMEM)
SMEM = pl.BlockSpec(memory_space=pltpu.SMEM)


def f32(*shape):
    return jax.ShapeDtypeStruct(shape, jnp.float32)


def vmem(*shape):
    return pltpu.VMEM(shape, jnp.float32)


def small_tables():
    return [pltpu.SMEM((N, N), jnp.int32), pltpu.SMEM((4,), jnp.float32), pltpu.SMEM((4,), jnp.float32), pltpu.SMEM((3,), jnp.float32)]


def params():
    return pltpu.CompilerParams(vmem_limit_bytes=32 * 1024 * 1024)


def swap(block, axis, parity):
    size = lax.axis_size(axis)
    route = []
    for i in range(parity, size - 1, 2):
        route += [(i, i + 1), (i + 1, i)]
    return lax.ppermute(block, axis, route)


def call_alone(inputs):
    plane = (2 * STEPS, N, NY)
    return pl.pallas_call(
        alone_kernel,
        out_shape=[f32(X_TILES, N, NY)] * 2 + [f32(OWN_TILES, N, NY)] * 2 + [f32(5, N, N, LANES), f32(19, N, LANES)],
        in_specs=[HBM] * 7,
        out_specs=[VMEM] * 6,
        scratch_shapes=[vmem(3, N, N, NY)] * 4
        + [vmem(*plane)] * 4
        + [vmem(4, 4, N, NY)]
        + small_tables()
        + [pltpu.SemaphoreType.DMA((8,))],
        compiler_params=params(),
        name="alone",
    )(*inputs)


def call_forward(r1, r0):
    return pl.pallas_call(
        forward_kernel,
        out_shape=[f32(FAR_TILES, N, NY)] * 2 + [f32(X_TILES, N, NY)] * 2 + [f32(7, N, NY)],
        in_specs=[VMEM] * 2,
        out_specs=[VMEM] * 5,
        scratch_shapes=[vmem(2, FAR_TILES, N, NY)],
        compiler_params=params(),
        name="forward",
    )(r1, r0)


def call_near(live, fields, coef, tables, received):
    state = f32(3, ROWS, 2, N, NY)
    return pl.pallas_call(
        functools.partial(near_kernel, live),
        out_shape=[state] * 4
        + [f32(5, ROWS, 2, N, LANES), f32(2, OWN_TILES, N, NY), f32(STEPS, 3, N, NY)],
        in_specs=[HBM] * 3 + [VMEM] * 7,
        out_specs=[VMEM] * 7,
        scratch_shapes=[pltpu.SemaphoreType.DMA((4,))],
        compiler_params=params(),
        cost_estimate=pl.CostEstimate(flops=20_000_000, bytes_accessed=20_000_000, transcendentals=0),
        name="near",
    )(*fields, coef, tables, *received)


def call_far(live, state, tables, received, weights):
    return pl.pallas_call(
        functools.partial(far_kernel, live),
        out_shape=[f32(3, N, N, NY), f32(3, N, N, NY), f32(2, 3, N, N, NY), f32(FREQS, 2, 3, 1, N, NY)],
        in_specs=[VMEM] * 13 + [SMEM],
        out_specs=[HBM] * 4,
        scratch_shapes=[vmem(3, ROWS, 2, N, NY)] * 4
        + [
            vmem(5, ROWS, 2, N, LANES),
            vmem(STEPS, 3, N, NY),
            vmem(2, FAR_TILES, N, NY),
            vmem(FREQS, 2, 3, 1, N, NY),
            pltpu.SemaphoreType.DMA((4 * N + 1,)),
        ],
        compiler_params=params(),
        name="far",
    )(*state, tables, *received, weights)


def on_device(e_field, h_field, polar, material, eps_table, loss_table, lorentz, freqs):
    inputs = (e_field, h_field, polar, material, eps_table, loss_table, lorentz)
    inputs = tuple(pltpu.with_memory_space_constraint(x, pltpu.HBM) for x in inputs)
    m0, m1, w0, w1, coef, tables = call_alone(inputs)
    r1 = swap(m1, "dev", 1)
    r0 = swap(m0, "dev", 0)
    g1 = swap(w1, "grp", 1)
    g0 = swap(w0, "grp", 0)
    v1, v0, high, low, ghosts = call_forward(r1, r0)
    f1 = swap(v1, "grp", 1)
    f0 = swap(v0, "grp", 0)
    angles = freqs * jnp.arange(1, STEPS + 1, dtype=jnp.float32)[:, None]
    weights = jnp.stack([jnp.cos(angles), -jnp.sin(angles)], axis=2)
    live = {}
    state = call_near(live, inputs[:3], coef, tables, (high, low, ghosts, g1, g0))
    return tuple(call_far(live, state, tables, (high, low, ghosts, f1, f0), weights))


def solution(mesh):
    placed = (
        P(None, "grp", "dev", None),
        P(None, "grp", "dev", None),
        P(None, None, "grp", "dev", None),
        P("grp", "dev"),
        P(),
        P(),
        P(),
        P(),
    )
    return jax.shard_map(
        on_device,
        mesh=mesh,
        in_specs=placed,
        out_specs=(
            P(None, "grp", "dev", None),
            P(None, "grp", "dev", None),
            P(None, None, "grp", "dev", None),
            P(None, None, None, "grp", "dev", None),
        ),
        check_vma=False,
    )
```

```python
import functools

import jax
import jax.numpy as jnp
from jax import lax
from jax.experimental import pallas as pl
from jax.experimental.pallas import tpu as pltpu
from jax.sharding import PartitionSpec as P


STEPS = 4
FREQS = 4
COURANT = 0.5
N = 8
NY = 640
LANES = 128

ROWS = 17
Z0 = 5

X_TILES = 12
OWN_TILES = 12
FAR_TILES = 7


def ladder(kind, c, first, count, start, way):
    return [(kind, first + i, c, start + way * j) for i in range(count) for j in range(count - i)]


def materials(places):
    return [("mat", 0, 0, x) for x in places]


def ray_rows(entries, tile, spare=()):
    free = [*spare, *((tile + k // N, k % N) for k in range(len(entries)))]
    return dict(zip(entries, free))


HIGH = (0, 1, 2)
LOW = (4, 5, 6, 7)
HX = ray_rows(
    ladder("ze", 0, 0, 3, 0, 1) + ladder("ze", 1, 0, 3, 0, 1) + ladder("zh", 0, 1, 3, 0, 1) + ladder("zh", 1, 1, 2, 0, 1) + materials(HIGH),
    8,
)
LX = ray_rows(
    ladder("ze", 0, 0, 4, 7, -1) + ladder("ze", 1, 0, 3, 7, -1) + ladder("zh", 0, 1, 3, 7, -1) + ladder("zh", 1, 1, 3, 7, -1) + materials(LOW),
    8,
)
HZ = ray_rows(
    ladder("xe", 0, 0, 3, 0, 1) + ladder("xe", 1, 0, 3, 0, 1) + ladder("xh", 0, 1, 2, 0, 1) + ladder("xh", 1, 1, 2, 0, 1), 9
)
LZ = ray_rows(
    ladder("xe", 0, 0, 3, 7, -1) + ladder("xe", 1, 0, 3, 7, -1) + ladder("xh", 0, 1, 3, 7, -1) + ladder("xh", 1, 1, 2, 7, -1), 9
)
HF = ray_rows(
    ladder("xhl", 0, 1, 2, 0, 1) + ladder("xhl", 1, 1, 3, 0, 1) + ladder("xeh", 0, 0, 3, 0, 1) + ladder("xeh", 1, 0, 3, 0, 1)
    + materials(HIGH + LOW),
    4,
    ((1, 3), (1, 4), (3, 2), (3, 5)),
)
LF = ray_rows(
    ladder("xhl", 0, 1, 3, 7, -1) + ladder("xhl", 1, 1, 3, 7, -1) + ladder("xeh", 0, 0, 3, 7, -1) + ladder("xeh", 1, 0, 4, 7, -1)
    + materials(HIGH + LOW),
    3,
    ((1, 2), (1, 4), (2, 5)),
)


def ghost_place(kind, n, c, x):
    if kind == "ze":
        return {0: (c, x), 3: (c, (x + 4) % N), 1: (2 + c, x), 2: (2 + c, (x + 4) % N)}[n]
    return {1: (c, x), 3: (c, (x + 4) % N), 2: (2, (x + 4 * c) % N)}[n]


def ghost_tile(ref, kind, n, c):
    tile, row = ghost_place(kind, n, c, 0)
    value = ref[tile]
    return pltpu.roll(value, 4, 0) if row == 4 else value


def slot_e(n, c):
    return 2 * n + c


def slot_h(n, c):
    return 2 * (n - 1) + c


def wide(tile):
    return jnp.concatenate([tile] * (NY // LANES), axis=1)


def sublane(shape):
    return lax.broadcasted_iota(jnp.int32, shape, 0)


def lane(shape):
    return lax.broadcasted_iota(jnp.int32, shape, 1)


def add(x, y):
    return y if x is None else x if y is None else x + y


def sub(x, y):
    return x if y is None else -y if x is None else x - y


def mul(k, x):
    return None if x is None else k * x


def y_ahead(v):
    if v is None:
        return None
    r = pltpu.roll(v, NY - 1, 1)
    last = r[:, NY - LANES :]
    return jnp.concatenate([r[:, : NY - LANES], jnp.where(lane(last.shape) == LANES - 1, 0.0, last)], axis=1)


def y_behind(v):
    if v is None:
        return None
    r = pltpu.roll(v, 1, 1)
    first = r[:, :LANES]
    return jnp.concatenate([jnp.where(lane(first.shape) == 0, 0.0, first), r[:, LANES:]], axis=1)


def x_up(v):
    return None if v is None else pltpu.roll(v, N - 1, 0)


def x_down(v):
    return None if v is None else pltpu.roll(v, 1, 0)


def choose(edge, x, y):
    if x is None and y is None:
        return None
    return jnp.where(edge, 0.0 if x is None else x, 0.0 if y is None else y)


def kind_tables(eps_ref, loss_ref):
    out = []
    for k in range(4):
        damping = jnp.full((N, LANES), loss_ref[k], jnp.float32)
        permittivity = jnp.full((N, LANES), eps_ref[k], jnp.float32)
        scale = 1.0 / (1.0 + damping)
        inverse = 1.0 / permittivity
        out.append(((1.0 - damping) * scale, COURANT * scale, COURANT * scale * inverse, inverse))
    return out


def row_coefficients(kind, tables):
    masks = [kind == k + 1.0 for k in range(4)]
    out = []
    for j in range(4):
        total = jnp.zeros((N, LANES), jnp.float32)
        for k in range(4):
            total = jnp.where(masks[k], tables[k][j], total)
        out.append(total)
    out.append(jnp.where(masks[3], 1.0, 0.0))
    return out


def polar_scalars(lorentz_ref):
    shape = (N, LANES)
    a = jnp.full(shape, lorentz_ref[0], jnp.float32)
    g = jnp.full(shape, lorentz_ref[1], jnp.float32)
    s = jnp.full(shape, lorentz_ref[2], jnp.float32)
    scale = 1.0 / (1.0 + 0.5 * g)
    return (1.0 - a * a - 0.5 * g) * scale, (1.0 - 0.5 * g) * scale, s * a * a * scale


def own_kinds(material_ref):
    row = sublane((N, LANES))
    out = []
    for z in range(N):
        kind = jnp.zeros((N, LANES), jnp.int32)
        for x in range(N):
            kind = jnp.where(row == x, material_ref[z, x] + 1, kind)
        out.append(kind.astype(jnp.float32))
    return out


def e_update(curl, e, a, b, k, polar):
    retain, _, e_gain, inverse, active = k
    p, q, r = polar
    moved = mul(active, add(sub(mul(p, a), mul(q, b)), mul(r, e)))
    e_new = sub(add(mul(retain, e), mul(e_gain, curl)), mul(inverse, moved))
    p_new = add(a, moved)
    if b is None:
        return e_new, mul(active, p_new)
    return e_new, jnp.where(active > 0.5, p_new, b)


def start_all(pairs, sems):
    copies = [pltpu.make_async_copy(source, target, sems.at[i]) for i, (source, target) in enumerate(pairs)]
    for copy in copies:
        copy.start()
    return copies


def wait_all(copies):
    for copy in copies:
        copy.wait()


def alone_kernel(
    e_hbm, h_hbm, p_hbm, material_hbm, eps_hbm, loss_hbm, lorentz_hbm,
    m0, m1, w0, w1, coef, shared,
    e, h, a, b, ze, zh, xe, xh, rays, material, eps, loss, lorentz, sems,
):
    high_first = lax.rem(lax.axis_index("dev"), 2) == 0
    above_first = lax.rem(lax.axis_index("grp"), 2) == 0
    small = start_all(
        [(material_hbm, material), (eps_hbm, eps), (loss_hbm, loss), (lorentz_hbm, lorentz)], sems.at[pl.ds(0, 4)]
    )
    large = start_all(
        [(e_hbm, e), (h_hbm, h), (p_hbm.at[0], a), (p_hbm.at[1], b)], sems.at[pl.ds(4, 4)]
    )
    wait_all(small)
    tables = kind_tables(eps, loss)
    polar = polar_scalars(lorentz)
    for i, v in enumerate([v for table in tables for v in table] + list(polar)):
        shared[i] = v
    polar = [wide(v) for v in polar]
    ln = lane((N, LANES))
    packed = jnp.zeros((N, LANES), jnp.float32)
    for z, kind in enumerate(own_kinds(material)):
        packed = jnp.where(ln == z, kind, packed)
        for j, v in enumerate(row_coefficients(kind, tables)):
            coef[j, z] = v
    packed = wide(packed)
    w0[8] = packed
    w1[8] = packed
    wait_all(large[:2])
    row = sublane((N, NY))
    top = row == N - 1
    bottom = row == 0

    for n in range(1, STEPS + 1):
        old, new = (a, b) if n % 2 == 1 else (b, a)
        for c in range(2):
            ze[slot_e(n - 1, c)] = e[c, 0]
        for z in range(N):
            k = [wide(coef[j, z]) for j in range(5)]
            retain, h_gain = k[0], k[1]
            ex, ey, ez = (e[c, z] for c in range(3))
            e1x, e1y = (e[c, z + 1] if z < N - 1 else None for c in range(2))
            r = slot_e(n - 1, 0)
            xe[z, r : r + 1, :] = ey[0:1, :]
            xe[z, r + 1 : r + 2, :] = ez[0:1, :]
            xa_y = choose(top, None, x_up(ey))
            xa_z = choose(top, None, x_up(ez))
            hx = retain * h[0, z] - h_gain * ((y_ahead(ez) - ez) - sub(e1y, ey))
            hy = retain * h[1, z] - h_gain * (sub(e1x, ex) - (xa_z - ez))
            hz = retain * h[2, z] - h_gain * ((xa_y - ey) - (y_ahead(ex) - ex))
            h[0, z] = hx
            h[1, z] = hy
            h[2, z] = hz
            r = slot_h(n, 0)
            xh[z, r : r + 1, :] = hy[N - 1 : N, :]
            xh[z, r + 1 : r + 2, :] = hz[N - 1 : N, :]
        if n == 1:
            wait_all(large[2:])
        for z in range(N if n < STEPS else 0):
            k = [wide(coef[j, z]) for j in range(5)]
            ex, ey, ez = (e[c, z] for c in range(3))
            hx, hy, hz = (h[c, z] for c in range(3))
            lx, ly = (h[c, z - 1] if z else None for c in range(2))
            xb_y = choose(bottom, None, x_down(hy))
            xb_z = choose(bottom, None, x_down(hz))
            curls = (
                (hz - y_behind(hz)) - sub(hy, ly),
                sub(hx, lx) - (hz - xb_z),
                (hy - xb_y) - (hx - y_behind(hx)),
            )
            for c, (curl, field) in enumerate(zip(curls, (ex, ey, ez))):
                e[c, z], new[c, z] = e_update(curl, field, old[c, z], new[c, z], k, polar)
        for c in range(2):
            zh[slot_h(n, c)] = h[c, N - 1]

    for i, table in enumerate((HX, LX)):
        for (kind, n, c, x), (tile, r) in table.items():
            if kind == "mat":
                source = w0.at[8]
            else:
                source = ze.at[slot_e(n, c)] if kind == "ze" else zh.at[slot_h(n, c)]
            rays[i, tile - 8, r : r + 1, :] = source[x : x + 1, :]
    for i, table in enumerate((HZ, LZ)):
        for (kind, n, c, z), (tile, r) in table.items():
            at = slot_e(n, c) if kind == "xe" else slot_h(n, c)
            source = xe if kind == "xe" else xh
            rays[2 + i, tile - 9, r : r + 1, :] = source[z, at : at + 1, :]

    def deal(first, one, other, tile, for_above, for_below):
        one[tile] = jnp.where(first, for_above, for_below)
        other[tile] = jnp.where(first, for_below, for_above)

    for i in range(N):
        deal(high_first, m0, m1, i, xh[i], xe[i])
        deal(above_first, w0, w1, i, zh[i], ze[i])
    for i in range(4):
        deal(high_first, m0, m1, 8 + i, rays[1, i], rays[0, i])
    for i in range(3):
        deal(above_first, w0, w1, 9 + i, rays[3, i], rays[2, i])


def forward_kernel(r1, r0, v1, v0, high, low, ghosts, rays):
    high_first = lax.rem(lax.axis_index("dev"), 2) == 0
    above_first = lax.rem(lax.axis_index("grp"), 2) == 0
    for i in range(X_TILES):
        one, other = r0[i], r1[i]
        high[i] = jnp.where(high_first, one, other)
        low[i] = jnp.where(high_first, other, one)
    for source, table in ((high, HX), (low, LX)):
        for (kind, n, c, x), (tile, r) in table.items():
            value = source[tile, r : r + 1, :]
            if kind == "mat":
                for i, far in enumerate((HF, LF)):
                    to, at = far[(kind, n, c, x)]
                    rays[i, to, at : at + 1, :] = value
            else:
                to, at = ghost_place(kind, n, c, x)
                rays[0 if kind == "ze" else 1, to, at : at + 1, :] = value
    for i, table in enumerate((HF, LF)):
        for (kind, n, c, z), (tile, r) in table.items():
            if kind != "mat":
                at = slot_e(n, c) if kind == "xeh" else slot_h(n, c)
                source = high if kind == "xeh" else low
                rays[i, tile, r : r + 1, :] = source[z, at : at + 1, :]
    for i in range(4):
        ghosts[i] = rays[0, i]
    for i in range(3):
        ghosts[4 + i] = rays[1, i]
    for i in range(FAR_TILES):
        below, above = rays[0, i], rays[1, i]
        v0[i] = jnp.where(above_first, above, below)
        v1[i] = jnp.where(above_first, below, above)


def h_inputs(c, z, s):
    if c == 0:
        return [(2, z, s), (1, z, s), (1, z + 1, s)], [("z", 1)]
    if c == 1:
        return [(0, z, s), (0, z + 1, s), (2, z, s), (2, z, 1 - s)], [("z", 0), ("x", 1)]
    return [(1, z, s), (1, z, 1 - s), (0, z, s)], [("x", 0)]


def e_inputs(c, z, s):
    if c == 0:
        return [(2, z, s), (1, z, s), (1, z - 1, s)], [("z", 1)]
    if c == 1:
        return [(0, z, s), (0, z - 1, s), (2, z, s), (2, z, 1 - s)], [("z", 0), ("x", 1)]
    return [(1, z, s), (1, z, 1 - s), (0, z, s)], [("x", 0)]


def x_source(kind, n, c, z):
    if 0 <= z < N:
        r = slot_e(n, c) if kind == "xeh" else slot_h(n, c)
        return {"xeh": ("high", z, r), "xhl": ("low", z, r)}.get(kind)
    near, far, place = (HZ, HF, z - N) if z >= N else (LZ, LF, z + N)
    for name, table in (("own", near), ("far", far)):
        if (kind, n, c, place) in table:
            return (name, 0 if z >= N else 1, *table[(kind, n, c, place)])
    return None


def z_source(kind, n, c, z, s):
    if s == 0:
        if (kind, z) == ("ze", N):
            return ("own", 0, slot_e(n, c))
        return ("own", 1, slot_h(n, c)) if (kind, z) == ("zh", -1) else None
    if (kind, z) in (("ze", N), ("zh", -1)) and any(k[:3] == (kind, n, c) for k in (*HX, *LX)):
        return ("far", 0 if z == N else 1, kind, n, c)
    if (kind, z) in (("ze", 0), ("zh", N - 1)) and n < STEPS - (kind == "ze") and (kind, n, c) != ("zh", STEPS - 1, 0):
        return ("ghosts", kind, n, c)
    return None


def sources(field, n, z, s, wanted):
    out = []
    for border, c in wanted:
        if field == "h":
            at = x_source("xe" if s else "xeh", n - 1, c, z) if border == "x" else z_source("ze", n - 1, c, z + 1, s)
        else:
            at = x_source("xh" if s else "xhl", n, c, z) if border == "x" else z_source("zh", n, c, z - 1, s)
        out.append(at)
    return [at for at in out if at is not None]


def plan():
    mine = {(c, z, 0) for c in range(3) for z in range(N)}
    need = {("h", STEPS): set(mine), ("e", STEPS): set(mine)}
    for n in range(STEPS, 0, -1):
        for key in need[("e", n)]:
            need[("h", n)] |= set(e_inputs(*key)[0])
        need[("e", n - 1)] = set(need[("e", n)])
        need[("h", n - 1)] = set(need[("h", n)])
        for key in need[("h", n)]:
            need[("e", n - 1)] |= set(h_inputs(*key)[0])
    late = {("e", 0): set(), ("h", 0): set()}
    for n in range(1, STEPS + 1):
        for field, other, inputs, back in (("h", "e", h_inputs, n - 1), ("e", "h", e_inputs, n)):
            late[(field, n)] = set()
            for key in need[(field, n)]:
                before, wanted = inputs(*key)
                c, z, s = key
                if (
                    (s == 1 and not 0 <= z < N)
                    or key in late[(field, n - 1)]
                    or any(k in late[(other, back)] for k in before)
                    or any(at[0] == "far" for at in sources(field, n, z, s, wanted))
                ):
                    late[(field, n)].add(key)
    return need, late


NEED, LATE = plan()
FIELDS = {"e": 0, "h": 1, 0: 2, 1: 3}


class Pass:
    def __init__(self, second, live, stores, coefs, polar, places, row):
        self.second, self.live, self.stores = second, live, stores
        self.coefs, self.polar, self.places = coefs, polar, places
        self.top, self.bottom = row == N - 1, row == 0
        self.memo = {}

    def once(self, key, make):
        if key not in self.memo:
            self.memo[key] = make()
        return self.memo[key]

    def store(self, field, c, z, s, n):
        late = n > 0 and (c, z, s) in LATE[("h" if field == "h" else "e", n)]
        return self.stores[late][FIELDS[field]]

    def get(self, field, c, z, s, n):
        key = (field, c, z, s)
        if self.live.get(key, STEPS + 1) > n:
            return None
        made = n if field in ("e", "h") else n - 1 if (n - 1) % 2 == field else n - 2
        return self.once((*key, n), lambda: self.store(field, c, z, s, made)[c, Z0 + z, s])

    def put(self, field, c, z, s, n, value):
        if value is None:
            return
        self.store(field, c, z, s, n)[c, Z0 + z, s] = value
        self.live.setdefault((field, c, z, s), n)
        self.memo[(field, c, z, s, n)] = value

    def source(self, at):
        if at is None:
            return None
        if at[0] == "ghosts" or len(at) == 5:
            ref = self.places[at[0]] if at[0] == "ghosts" else self.places["far"].at[at[1]]
            kind, n, c = at[-3:]
            if at[0] == "ghosts" and kind == "zh":
                ref = ref.at[pl.ds(4, 3)]
            return ghost_tile(ref, kind, n, c)
        ref = self.places[at[0]]
        if at[0] in ("high", "low"):
            return ref[at[1], at[2] : at[2] + 1, :]
        if len(at) == 3:
            return ref[at[1], at[2]]
        return ref[at[1], at[2], at[3] : at[3] + 1, :]

    def k(self, j, z, s):
        coef = self.coefs[s == 1 and not 0 <= z < N]
        return self.once(("k", j, z, s), lambda: wide(coef[j, Z0 + z, s]))

    def x_neighbour(self, field, c, z, s, n):
        shift, edge = (x_up, self.top) if field == "e" else (x_down, self.bottom)

        def moved(half):
            return self.once(("x", field, c, z, half, n), lambda: shift(self.get(field, c, z, half, n)))

        kinds = ("xeh", "xe") if field == "e" else ("xhl", "xh")
        from_block = self.source(x_source(kinds[s], n, c - 1, z))
        return choose(edge, add(moved(1 - s), from_block), moved(s))

    def y_neighbour(self, field, c, z, s, n):
        shift = y_ahead if field == "e" else y_behind
        return self.once(("y", field, c, z, s, n), lambda: shift(self.get(field, c, z, s, n)))

    def z_neighbour(self, field, c, z, s, n):
        kind, at = ("ze", z + 1) if field == "e" else ("zh", z - 1)
        return add(self.get(field, c, at, s, n), self.source(z_source(kind, n, c, at, s)))

    def step_h(self, n, c, z, s):
        m = n - 1
        ex, ey, ez = (lambda c=c: self.get("e", c, z, s, m) for c in range(3))
        if c == 0:
            curl = sub(sub(self.y_neighbour("e", 2, z, s, m), ez()), sub(self.z_neighbour("e", 1, z, s, m), ey()))
        elif c == 1:
            curl = sub(sub(self.z_neighbour("e", 0, z, s, m), ex()), sub(self.x_neighbour("e", 2, z, s, m), ez()))
        else:
            curl = sub(sub(self.x_neighbour("e", 1, z, s, m), ey()), sub(self.y_neighbour("e", 0, z, s, m), ex()))
        value = sub(mul(self.k(0, z, s), self.get("h", c, z, s, m)), mul(self.k(1, z, s), curl))
        self.put("h", c, z, s, n, value)

    def step_e(self, n, c, z, s):
        hx, hy, hz = (lambda c=c: self.get("h", c, z, s, n) for c in range(3))
        if c == 0:
            curl = sub(sub(hz(), self.y_neighbour("h", 2, z, s, n)), sub(hy(), self.z_neighbour("h", 1, z, s, n)))
        elif c == 1:
            curl = sub(sub(hx(), self.z_neighbour("h", 0, z, s, n)), sub(hz(), self.x_neighbour("h", 2, z, s, n)))
        else:
            curl = sub(sub(hy(), self.x_neighbour("h", 1, z, s, n)), sub(hx(), self.y_neighbour("h", 0, z, s, n)))
        old, new = (n - 1) % 2, n % 2
        k = [self.k(j, z, s) for j in range(5)]
        e_new, p_new = e_update(
            curl, self.get("e", c, z, s, n - 1), self.get(old, c, z, s, n), self.get(new, c, z, s, n), k, self.polar
        )
        self.put("e", c, z, s, n, e_new)
        if n < STEPS or s == 0:
            self.put(new, c, z, s, n, p_new)

    def row(self, n, z, seen, field):
        step = self.step_h if field == "h" else self.step_e
        for s in range(2):
            for c in range(3):
                if (c, z, s) in NEED[(field, n)] and ((c, z, s) in LATE[(field, n)]) == self.second:
                    step(n, c, z, s)
                    if field == "e" and (z, s) == (N // 2, 0):
                        seen[n - 1, c] = self.get("e", c, z, s, n)
        self.memo = {}


def near_kernel(
    live, e_hbm, h_hbm, p_hbm, coef_in, tables, high, low, ghosts, g1, g0,
    e, h, a, b, coef, own, seen,
    side, sems,
):
    above_first = lax.rem(lax.axis_index("grp"), 2) == 0
    mine = pl.ds(Z0, N)
    large = start_all(
        [
            (e_hbm, e.at[:, mine, 0]),
            (h_hbm, h.at[:, mine, 0]),
            (p_hbm.at[0], a.at[:, mine, 0]),
            (p_hbm.at[1], b.at[:, mine, 0]),
        ],
        sems,
    )
    for i in range(OWN_TILES):
        x, y = g0[i], g1[i]
        own[0, i] = jnp.where(above_first, x, y)
        own[1, i] = jnp.where(above_first, y, x)
    ghost_materials(side, [(high, HX, HIGH), (low, LX, LOW)])
    columns = [(z, 1, side[...], z) for z in range(N)]
    columns += [(z, 0, own[1 if z < 0 else 0, 8, :, 0:LANES], z % N) for z in (*range(-4, 0), *range(N, N + 3))]
    fill_coefficients(coef, columns, tables)
    for z in range(N):
        for j in range(5):
            coef[j, Z0 + z, 0] = coef_in[j, z]
    polar = [wide(tables[16 + j]) for j in range(3)]
    wait_all(large)
    live.update({(field, c, z, 0): 0 for field in FIELDS for c in range(3) for z in range(N)})
    places = {"own": own, "high": high, "low": low, "ghosts": ghosts}
    run = Pass(False, live, [(e, h, a, b)] * 2, [coef, None], polar, places, sublane((N, NY)))
    for n in range(1, STEPS + 1):
        for z in range(-4, N + 3):
            run.row(n, z, seen, "h")
        for z in range(-4, N + 3):
            run.row(n, z, seen, "e")


def ghost_materials(tile, found):
    tile[...] = jnp.zeros((N, LANES), jnp.float32)
    for source, table, places in found:
        for x in places:
            t, r = table[("mat", 0, 0, x)]
            tile[x : x + 1, :] = source[t, r : r + 1, 0:LANES]


def fill_coefficients(coef, columns, tables):
    stacked = [[tables[4 * k + j] for j in range(4)] for k in range(4)]
    for z, s, tile, at in columns:
        kind = jnp.broadcast_to(tile[:, at : at + 1], (N, LANES))
        for j, v in enumerate(row_coefficients(kind, stacked)):
            coef[j, Z0 + z, s] = v


def far_kernel(
    live, e_in, h_in, a_in, b_in, coef_in, own, seen_in, tables, high, low, ghosts, f1, f0, weights,
    e_out, h_out, p_out, s_out,
    e, h, a, b, coef, seen, far, corners, spectrum, sems,
):
    above_first = lax.rem(lax.axis_index("grp"), 2) == 0
    for i in range(FAR_TILES):
        x, y = f0[i], f1[i]
        far[0, i] = jnp.where(above_first, x, y)
        far[1, i] = jnp.where(above_first, y, x)
    for i, table in enumerate((HF, LF)):
        ghost_materials(corners.at[i], [(far.at[i], table, HIGH + LOW)])
    columns = [(z, 1, corners[1 if z < 0 else 0], z % N) for z in (*range(-4, 0), *range(N, N + 3))]
    fill_coefficients(coef, columns, tables)
    polar = [wide(tables[16 + j]) for j in range(3)]
    places = {"own": own, "far": far, "high": high, "low": low, "ghosts": ghosts}
    run = Pass(True, live, [(e_in, h_in, a_in, b_in), (e, h, a, b)], [coef_in, coef], polar, places, sublane((N, NY)))
    for field, n, last, made in ((0, STEPS, a, a_in), (1, STEPS - 1, b, b_in), ("e", STEPS, e, e_in), ("h", STEPS, h, h_in)):
        for c in range(3):
            for z in range(N):
                if (c, z, 0) not in LATE[("h" if field == "h" else "e", n)]:
                    last[c, Z0 + z, 0] = made[c, Z0 + z, 0]
    outs = []
    for n in range(1, STEPS + 1):
        if n == STEPS:
            outs += start_all([(b.at[:, pl.ds(Z0, N), 0], p_out.at[1])], sems.at[pl.ds(1, 1)])
        for z in range(-4, N + 3):
            run.row(n, z, seen, "h")
        if n == STEPS:
            outs += start_all([(h.at[:, pl.ds(Z0, N), 0], h_out)], sems.at[pl.ds(0, 1)])
            order = [*range(N // 2, N), *range(N // 2)]
        else:
            order = range(-4, N + 3)
        for z in order:
            run.row(n, z, seen, "e")
            if n == STEPS:
                if z % 4 == 3:
                    at, to = pl.ds(Z0 + z - 3, 4), pl.ds(z - 3, 4)
                    outs += start_all(
                        [(e.at[:, at, 0], e_out.at[:, to]), (a.at[:, at, 0], p_out.at[0, :, to])],
                        sems.at[pl.ds(3 + z // 4 * 2, 2)],
                    )
                if z == N // 2:
                    for c in range(3):
                        planes = [
                            (seen if (c, z, 0) in LATE[("e", i + 1)] else seen_in)[i, c] for i in range(STEPS)
                        ]
                        for f in range(FREQS):
                            for q in range(2):
                                total = wide(weights[2 * f + q]) * planes[0]
                                for i in range(1, STEPS):
                                    total = total + wide(weights[2 * FREQS * i + 2 * f + q]) * planes[i]
                                spectrum[f, q, c, 0] = total
                    outs += start_all([(spectrum, s_out)], sems.at[pl.ds(2, 1)])
    wait_all(outs)


HBM = pl.BlockSpec(memory_space=pltpu.HBM)
VMEM = pl.BlockSpec(memory_space=pltpu.VMEM)
SMEM = pl.BlockSpec(memory_space=pltpu.SMEM)


def f32(*shape):
    return jax.ShapeDtypeStruct(shape, jnp.float32)


def vmem(*shape):
    return pltpu.VMEM(shape, jnp.float32)


def small_tables():
    return [pltpu.SMEM((N, N), jnp.int32), pltpu.SMEM((4,), jnp.float32), pltpu.SMEM((4,), jnp.float32), pltpu.SMEM((3,), jnp.float32)]


def params():
    return pltpu.CompilerParams(vmem_limit_bytes=32 * 1024 * 1024)


def swap(block, axis, parity):
    size = lax.axis_size(axis)
    route = []
    for i in range(parity, size - 1, 2):
        route += [(i, i + 1), (i + 1, i)]
    return lax.ppermute(block, axis, route)


def call_alone(inputs):
    plane = (2 * STEPS, N, NY)
    return pl.pallas_call(
        alone_kernel,
        out_shape=[f32(X_TILES, N, NY)] * 2 + [f32(OWN_TILES, N, NY)] * 2 + [f32(5, N, N, LANES), f32(19, N, LANES)],
        in_specs=[HBM] * 7,
        out_specs=[VMEM] * 6,
        scratch_shapes=[vmem(3, N, N, NY)] * 4
        + [vmem(*plane)] * 4
        + [vmem(4, 4, N, NY)]
        + small_tables()
        + [pltpu.SemaphoreType.DMA((8,))],
        compiler_params=params(),
        name="alone",
    )(*inputs)


def call_forward(r1, r0):
    return pl.pallas_call(
        forward_kernel,
        out_shape=[f32(FAR_TILES, N, NY)] * 2 + [f32(X_TILES, N, NY)] * 2 + [f32(7, N, NY)],
        in_specs=[VMEM] * 2,
        out_specs=[VMEM] * 5,
        scratch_shapes=[vmem(2, FAR_TILES, N, NY)],
        compiler_params=params(),
        name="forward",
    )(r1, r0)


def call_near(live, fields, coef, tables, received):
    state = f32(3, ROWS, 2, N, NY)
    return pl.pallas_call(
        functools.partial(near_kernel, live),
        out_shape=[state] * 4
        + [f32(5, ROWS, 2, N, LANES), f32(2, OWN_TILES, N, NY), f32(STEPS, 3, N, NY)],
        in_specs=[HBM] * 3 + [VMEM] * 7,
        out_specs=[VMEM] * 7,
        scratch_shapes=[vmem(N, LANES), pltpu.SemaphoreType.DMA((4,))],
        compiler_params=params(),
        cost_estimate=pl.CostEstimate(flops=20_000_000, bytes_accessed=20_000_000, transcendentals=0),
        name="near",
    )(*fields, coef, tables, *received)


def call_far(live, state, tables, received, weights):
    return pl.pallas_call(
        functools.partial(far_kernel, live),
        out_shape=[f32(3, N, N, NY), f32(3, N, N, NY), f32(2, 3, N, N, NY), f32(FREQS, 2, 3, 1, N, NY)],
        in_specs=[VMEM] * 14,
        out_specs=[HBM] * 4,
        scratch_shapes=[vmem(3, ROWS, 2, N, NY)] * 4
        + [
            vmem(5, ROWS, 2, N, LANES),
            vmem(STEPS, 3, N, NY),
            vmem(2, FAR_TILES, N, NY),
            vmem(2, N, LANES),
            vmem(FREQS, 2, 3, 1, N, NY),
            pltpu.SemaphoreType.DMA((7,)),
        ],
        compiler_params=params(),
        name="far",
    )(*state, tables, *received, weights)


def on_device(e_field, h_field, polar, material, eps_table, loss_table, lorentz, freqs):
    inputs = (e_field, h_field, polar, material, eps_table, loss_table, lorentz)
    inputs = tuple(pltpu.with_memory_space_constraint(x, pltpu.HBM) for x in inputs)
    m0, m1, w0, w1, coef, tables = call_alone(inputs)
    r1 = swap(m1, "dev", 1)
    r0 = swap(m0, "dev", 0)
    g1 = swap(w1, "grp", 1)
    g0 = swap(w0, "grp", 0)
    v1, v0, high, low, ghosts = call_forward(r1, r0)
    f1 = swap(v1, "grp", 1)
    f0 = swap(v0, "grp", 0)
    angles = freqs * jnp.arange(1, STEPS + 1, dtype=jnp.float32)[:, None]
    weights = jnp.stack([jnp.cos(angles), -jnp.sin(angles)], axis=2)
    weights = jnp.broadcast_to(weights.reshape(-1, 1, 1), (2 * FREQS * STEPS, N, LANES))
    live = {}
    state = call_near(live, inputs[:3], coef, tables, (high, low, ghosts, g1, g0))
    return tuple(call_far(live, state, tables, (high, low, ghosts, f1, f0), weights))


def solution(mesh):
    placed = (
        P(None, "grp", "dev", None),
        P(None, "grp", "dev", None),
        P(None, None, "grp", "dev", None),
        P("grp", "dev"),
        P(),
        P(),
        P(),
        P(),
    )
    return jax.shard_map(
        on_device,
        mesh=mesh,
        in_specs=placed,
        out_specs=(
            P(None, "grp", "dev", None),
            P(None, "grp", "dev", None),
            P(None, None, "grp", "dev", None),
            P(None, None, None, "grp", "dev", None),
        ),
        check_vma=False,
    )
```

```python
import functools

import jax
import jax.numpy as jnp
from jax import lax
from jax.experimental import pallas as pl
from jax.experimental.pallas import tpu as pltpu
from jax.sharding import PartitionSpec as P


STEPS = 4
FREQS = 4
COURANT = 0.5
N = 8
NY = 640
LANES = 128

ROWS = 17
Z0 = 5

X_TILES = 12
OWN_TILES = 12
FAR_TILES = 7


def ladder(kind, c, first, count, start, way):
    return [(kind, first + i, c, start + way * j) for i in range(count) for j in range(count - i)]


def materials(places):
    return [("mat", 0, 0, x) for x in places]


def ray_rows(entries, tile, spare=()):
    free = [*spare, *((tile + k // N, k % N) for k in range(len(entries)))]
    return dict(zip(entries, free))


HIGH = (0, 1, 2)
LOW = (4, 5, 6, 7)
HX = ray_rows(
    ladder("ze", 0, 0, 3, 0, 1) + ladder("ze", 1, 0, 3, 0, 1) + ladder("zh", 0, 1, 3, 0, 1) + ladder("zh", 1, 1, 2, 0, 1) + materials(HIGH),
    8,
)
LX = ray_rows(
    ladder("ze", 0, 0, 4, 7, -1) + ladder("ze", 1, 0, 3, 7, -1) + ladder("zh", 0, 1, 3, 7, -1) + ladder("zh", 1, 1, 3, 7, -1) + materials(LOW),
    8,
)
HZ = ray_rows(
    ladder("xe", 0, 0, 3, 0, 1) + ladder("xe", 1, 0, 3, 0, 1) + ladder("xh", 0, 1, 2, 0, 1) + ladder("xh", 1, 1, 2, 0, 1), 9
)
LZ = ray_rows(
    ladder("xe", 0, 0, 3, 7, -1) + ladder("xe", 1, 0, 3, 7, -1) + ladder("xh", 0, 1, 3, 7, -1) + ladder("xh", 1, 1, 2, 7, -1), 9
)
HF = ray_rows(
    ladder("xhl", 0, 1, 2, 0, 1) + ladder("xhl", 1, 1, 3, 0, 1) + ladder("xeh", 0, 0, 3, 0, 1) + ladder("xeh", 1, 0, 3, 0, 1)
    + materials(HIGH + LOW),
    4,
    ((1, 3), (1, 4), (3, 2), (3, 5)),
)
LF = ray_rows(
    ladder("xhl", 0, 1, 3, 7, -1) + ladder("xhl", 1, 1, 3, 7, -1) + ladder("xeh", 0, 0, 3, 7, -1) + ladder("xeh", 1, 0, 4, 7, -1)
    + materials(HIGH + LOW),
    3,
    ((1, 2), (1, 4), (2, 5)),
)


def ghost_place(kind, n, c, x):
    if kind == "ze":
        return {0: (c, x), 3: (c, (x + 4) % N), 1: (2 + c, x), 2: (2 + c, (x + 4) % N)}[n]
    return {1: (c, x), 3: (c, (x + 4) % N), 2: (2, (x + 4 * c) % N)}[n]


def ghost_tile(ref, kind, n, c):
    tile, row = ghost_place(kind, n, c, 0)
    value = ref[tile]
    return pltpu.roll(value, 4, 0) if row == 4 else value


def slot_e(n, c):
    return 2 * n + c


def slot_h(n, c):
    return 2 * (n - 1) + c


def wide(tile):
    return jnp.concatenate([tile] * (NY // LANES), axis=1)


def sublane(shape):
    return lax.broadcasted_iota(jnp.int32, shape, 0)


def lane(shape):
    return lax.broadcasted_iota(jnp.int32, shape, 1)


def add(x, y):
    return y if x is None else x if y is None else x + y


def sub(x, y):
    return x if y is None else -y if x is None else x - y


def mul(k, x):
    return None if x is None else k * x


def y_ahead(v):
    if v is None:
        return None
    r = pltpu.roll(v, NY - 1, 1)
    last = r[:, NY - LANES :]
    return jnp.concatenate([r[:, : NY - LANES], jnp.where(lane(last.shape) == LANES - 1, 0.0, last)], axis=1)


def y_behind(v):
    if v is None:
        return None
    r = pltpu.roll(v, 1, 1)
    first = r[:, :LANES]
    return jnp.concatenate([jnp.where(lane(first.shape) == 0, 0.0, first), r[:, LANES:]], axis=1)


def x_up(v):
    return None if v is None else pltpu.roll(v, N - 1, 0)


def x_down(v):
    return None if v is None else pltpu.roll(v, 1, 0)


def choose(edge, x, y):
    if x is None and y is None:
        return None
    return jnp.where(edge, 0.0 if x is None else x, 0.0 if y is None else y)


def kind_tables(eps_ref, loss_ref):
    out = []
    for k in range(4):
        damping = jnp.full((N, LANES), loss_ref[k], jnp.float32)
        permittivity = jnp.full((N, LANES), eps_ref[k], jnp.float32)
        scale = 1.0 / (1.0 + damping)
        inverse = 1.0 / permittivity
        out.append(((1.0 - damping) * scale, COURANT * scale, COURANT * scale * inverse, inverse))
    return out


def row_coefficients(kind, tables):
    masks = [kind == k + 1.0 for k in range(4)]
    out = []
    for j in range(4):
        total = jnp.zeros((N, LANES), jnp.float32)
        for k in range(4):
            total = jnp.where(masks[k], tables[k][j], total)
        out.append(total)
    out.append(jnp.where(masks[3], 1.0, 0.0))
    return out


def polar_scalars(lorentz_ref):
    shape = (N, LANES)
    a = jnp.full(shape, lorentz_ref[0], jnp.float32)
    g = jnp.full(shape, lorentz_ref[1], jnp.float32)
    s = jnp.full(shape, lorentz_ref[2], jnp.float32)
    scale = 1.0 / (1.0 + 0.5 * g)
    return (1.0 - a * a - 0.5 * g) * scale, (1.0 - 0.5 * g) * scale, s * a * a * scale


def own_kinds(material_ref):
    row = sublane((N, LANES))
    out = []
    for z in range(N):
        kind = jnp.zeros((N, LANES), jnp.int32)
        for x in range(N):
            kind = jnp.where(row == x, material_ref[z, x] + 1, kind)
        out.append(kind.astype(jnp.float32))
    return out


def e_update(curl, e, a, b, k, polar):
    retain, _, e_gain, inverse, active = k
    p, q, r = polar
    moved = mul(active, add(sub(mul(p, a), mul(q, b)), mul(r, e)))
    e_new = sub(add(mul(retain, e), mul(e_gain, curl)), mul(inverse, moved))
    p_new = add(a, moved)
    if b is None:
        return e_new, mul(active, p_new)
    return e_new, jnp.where(active > 0.5, p_new, b)


def start_all(pairs, sems):
    copies = [pltpu.make_async_copy(source, target, sems.at[i]) for i, (source, target) in enumerate(pairs)]
    for copy in copies:
        copy.start()
    return copies


def wait_all(copies):
    for copy in copies:
        copy.wait()


def alone_kernel(
    e_hbm, h_hbm, p_hbm, material_hbm, eps_hbm, loss_hbm, lorentz_hbm,
    m0, m1, w0, w1, coef, shared,
    e, h, a, b, ze, zh, xe, xh, rays, material, eps, loss, lorentz, sems,
):
    high_first = lax.rem(lax.axis_index("dev"), 2) == 0
    above_first = lax.rem(lax.axis_index("grp"), 2) == 0
    small = start_all(
        [(material_hbm, material), (eps_hbm, eps), (loss_hbm, loss), (lorentz_hbm, lorentz)], sems.at[pl.ds(0, 4)]
    )
    large = start_all(
        [(e_hbm, e), (h_hbm, h), (p_hbm.at[0], a), (p_hbm.at[1], b)], sems.at[pl.ds(4, 4)]
    )
    wait_all(small)
    tables = kind_tables(eps, loss)
    polar = polar_scalars(lorentz)
    for i, v in enumerate([v for table in tables for v in table] + list(polar)):
        shared[i] = v
    polar = [wide(v) for v in polar]
    ln = lane((N, LANES))
    packed = jnp.zeros((N, LANES), jnp.float32)
    for z, kind in enumerate(own_kinds(material)):
        packed = jnp.where(ln == z, kind, packed)
        for j, v in enumerate(row_coefficients(kind, tables)):
            coef[j, z] = v
    packed = wide(packed)
    w0[8] = packed
    w1[8] = packed
    wait_all(large[:2])
    row = sublane((N, NY))
    top = row == N - 1
    bottom = row == 0

    for n in range(1, STEPS + 1):
        old, new = (a, b) if n % 2 == 1 else (b, a)
        for c in range(2):
            ze[slot_e(n - 1, c)] = e[c, 0]
        for z in range(N):
            k = [wide(coef[j, z]) for j in range(5)]
            retain, h_gain = k[0], k[1]
            ex, ey, ez = (e[c, z] for c in range(3))
            e1x, e1y = (e[c, z + 1] if z < N - 1 else None for c in range(2))
            r = slot_e(n - 1, 0)
            xe[z, r : r + 1, :] = ey[0:1, :]
            xe[z, r + 1 : r + 2, :] = ez[0:1, :]
            xa_y = choose(top, None, x_up(ey))
            xa_z = choose(top, None, x_up(ez))
            hx = retain * h[0, z] - h_gain * ((y_ahead(ez) - ez) - sub(e1y, ey))
            hy = retain * h[1, z] - h_gain * (sub(e1x, ex) - (xa_z - ez))
            hz = retain * h[2, z] - h_gain * ((xa_y - ey) - (y_ahead(ex) - ex))
            h[0, z] = hx
            h[1, z] = hy
            h[2, z] = hz
            r = slot_h(n, 0)
            xh[z, r : r + 1, :] = hy[N - 1 : N, :]
            xh[z, r + 1 : r + 2, :] = hz[N - 1 : N, :]
        if n == 1:
            wait_all(large[2:])
        for z in range(N if n < STEPS else 0):
            k = [wide(coef[j, z]) for j in range(5)]
            ex, ey, ez = (e[c, z] for c in range(3))
            hx, hy, hz = (h[c, z] for c in range(3))
            lx, ly = (h[c, z - 1] if z else None for c in range(2))
            xb_y = choose(bottom, None, x_down(hy))
            xb_z = choose(bottom, None, x_down(hz))
            curls = (
                (hz - y_behind(hz)) - sub(hy, ly),
                sub(hx, lx) - (hz - xb_z),
                (hy - xb_y) - (hx - y_behind(hx)),
            )
            for c, (curl, field) in enumerate(zip(curls, (ex, ey, ez))):
                e[c, z], new[c, z] = e_update(curl, field, old[c, z], new[c, z], k, polar)
        for c in range(2):
            zh[slot_h(n, c)] = h[c, N - 1]

    for i, table in enumerate((HX, LX)):
        for (kind, n, c, x), (tile, r) in table.items():
            if kind == "mat":
                source = w0.at[8]
            else:
                source = ze.at[slot_e(n, c)] if kind == "ze" else zh.at[slot_h(n, c)]
            rays[i, tile - 8, r : r + 1, :] = source[x : x + 1, :]
    for i, table in enumerate((HZ, LZ)):
        for (kind, n, c, z), (tile, r) in table.items():
            at = slot_e(n, c) if kind == "xe" else slot_h(n, c)
            source = xe if kind == "xe" else xh
            rays[2 + i, tile - 9, r : r + 1, :] = source[z, at : at + 1, :]

    def deal(first, one, other, tile, for_above, for_below):
        one[tile] = jnp.where(first, for_above, for_below)
        other[tile] = jnp.where(first, for_below, for_above)

    for i in range(N):
        deal(high_first, m0, m1, i, xh[i], xe[i])
        deal(above_first, w0, w1, i, zh[i], ze[i])
    for i in range(4):
        deal(high_first, m0, m1, 8 + i, rays[1, i], rays[0, i])
    for i in range(3):
        deal(above_first, w0, w1, 9 + i, rays[3, i], rays[2, i])


def forward_kernel(r1, r0, v1, v0, high, low, ghosts, rays):
    high_first = lax.rem(lax.axis_index("dev"), 2) == 0
    above_first = lax.rem(lax.axis_index("grp"), 2) == 0
    for i in range(X_TILES):
        one, other = r0[i], r1[i]
        high[i] = jnp.where(high_first, one, other)
        low[i] = jnp.where(high_first, other, one)
    for source, table in ((high, HX), (low, LX)):
        for (kind, n, c, x), (tile, r) in table.items():
            value = source[tile, r : r + 1, :]
            if kind == "mat":
                for i, far in enumerate((HF, LF)):
                    to, at = far[(kind, n, c, x)]
                    rays[i, to, at : at + 1, :] = value
            else:
                to, at = ghost_place(kind, n, c, x)
                rays[0 if kind == "ze" else 1, to, at : at + 1, :] = value
    for i, table in enumerate((HF, LF)):
        for (kind, n, c, z), (tile, r) in table.items():
            if kind != "mat":
                at = slot_e(n, c) if kind == "xeh" else slot_h(n, c)
                source = high if kind == "xeh" else low
                rays[i, tile, r : r + 1, :] = source[z, at : at + 1, :]
    for i in range(4):
        ghosts[i] = rays[0, i]
    for i in range(3):
        ghosts[4 + i] = rays[1, i]
    for i in range(FAR_TILES):
        below, above = rays[0, i], rays[1, i]
        v0[i] = jnp.where(above_first, above, below)
        v1[i] = jnp.where(above_first, below, above)


def h_inputs(c, z, s):
    if c == 0:
        return [(2, z, s), (1, z, s), (1, z + 1, s)], [("z", 1)]
    if c == 1:
        return [(0, z, s), (0, z + 1, s), (2, z, s), (2, z, 1 - s)], [("z", 0), ("x", 1)]
    return [(1, z, s), (1, z, 1 - s), (0, z, s)], [("x", 0)]


def e_inputs(c, z, s):
    if c == 0:
        return [(2, z, s), (1, z, s), (1, z - 1, s)], [("z", 1)]
    if c == 1:
        return [(0, z, s), (0, z - 1, s), (2, z, s), (2, z, 1 - s)], [("z", 0), ("x", 1)]
    return [(1, z, s), (1, z, 1 - s), (0, z, s)], [("x", 0)]


def x_source(kind, n, c, z):
    if 0 <= z < N:
        r = slot_e(n, c) if kind == "xeh" else slot_h(n, c)
        return {"xeh": ("high", z, r), "xhl": ("low", z, r)}.get(kind)
    near, far, place = (HZ, HF, z - N) if z >= N else (LZ, LF, z + N)
    for name, table in (("own", near), ("far", far)):
        if (kind, n, c, place) in table:
            return (name, 0 if z >= N else 1, *table[(kind, n, c, place)])
    return None


def z_source(kind, n, c, z, s):
    if s == 0:
        if (kind, z) == ("ze", N):
            return ("own", 0, slot_e(n, c))
        return ("own", 1, slot_h(n, c)) if (kind, z) == ("zh", -1) else None
    if (kind, z) in (("ze", N), ("zh", -1)) and any(k[:3] == (kind, n, c) for k in (*HX, *LX)):
        return ("far", 0 if z == N else 1, kind, n, c)
    if (kind, z) in (("ze", 0), ("zh", N - 1)) and n < STEPS - (kind == "ze") and (kind, n, c) != ("zh", STEPS - 1, 0):
        return ("ghosts", kind, n, c)
    return None


def sources(field, n, z, s, wanted):
    out = []
    for border, c in wanted:
        if field == "h":
            at = x_source("xe" if s else "xeh", n - 1, c, z) if border == "x" else z_source("ze", n - 1, c, z + 1, s)
        else:
            at = x_source("xh" if s else "xhl", n, c, z) if border == "x" else z_source("zh", n, c, z - 1, s)
        out.append(at)
    return [at for at in out if at is not None]


def plan():
    mine = {(c, z, 0) for c in range(3) for z in range(N)}
    need = {("h", STEPS): set(mine), ("e", STEPS): set(mine)}
    for n in range(STEPS, 0, -1):
        for key in need[("e", n)]:
            need[("h", n)] |= set(e_inputs(*key)[0])
        need[("e", n - 1)] = set(need[("e", n)])
        need[("h", n - 1)] = set(need[("h", n)])
        for key in need[("h", n)]:
            need[("e", n - 1)] |= set(h_inputs(*key)[0])
    late = {("e", 0): set(), ("h", 0): set()}
    for n in range(1, STEPS + 1):
        for field, other, inputs, back in (("h", "e", h_inputs, n - 1), ("e", "h", e_inputs, n)):
            late[(field, n)] = set()
            for key in need[(field, n)]:
                before, wanted = inputs(*key)
                c, z, s = key
                if (
                    (s == 1 and not 0 <= z < N)
                    or key in late[(field, n - 1)]
                    or any(k in late[(other, back)] for k in before)
                    or any(at[0] == "far" for at in sources(field, n, z, s, wanted))
                ):
                    late[(field, n)].add(key)
    return need, late


NEED, LATE = plan()
FIELDS = {"e": 0, "h": 1, 0: 2, 1: 3}


class Pass:
    def __init__(self, second, live, stores, coefs, polar, places, row):
        self.second, self.live, self.stores = second, live, stores
        self.coefs, self.polar, self.places = coefs, polar, places
        self.top, self.bottom = row == N - 1, row == 0
        self.memo = {}

    def once(self, key, make):
        if key not in self.memo:
            self.memo[key] = make()
        return self.memo[key]

    def store(self, field, c, z, s, n):
        late = n > 0 and (c, z, s) in LATE[("h" if field == "h" else "e", n)]
        return self.stores[late][FIELDS[field]]

    def get(self, field, c, z, s, n):
        key = (field, c, z, s)
        if self.live.get(key, STEPS + 1) > n:
            return None
        made = n if field in ("e", "h") else n - 1 if (n - 1) % 2 == field else n - 2
        return self.once((*key, n), lambda: self.store(field, c, z, s, made)[c, Z0 + z, s])

    def put(self, field, c, z, s, n, value):
        if value is None:
            return
        self.store(field, c, z, s, n)[c, Z0 + z, s] = value
        self.live.setdefault((field, c, z, s), n)
        self.memo[(field, c, z, s, n)] = value

    def source(self, at):
        if at is None:
            return None
        if at[0] == "ghosts" or len(at) == 5:
            ref = self.places[at[0]] if at[0] == "ghosts" else self.places["far"].at[at[1]]
            kind, n, c = at[-3:]
            if at[0] == "ghosts" and kind == "zh":
                ref = ref.at[pl.ds(4, 3)]
            return ghost_tile(ref, kind, n, c)
        ref = self.places[at[0]]
        if at[0] in ("high", "low"):
            return ref[at[1], at[2] : at[2] + 1, :]
        if len(at) == 3:
            return ref[at[1], at[2]]
        return ref[at[1], at[2], at[3] : at[3] + 1, :]

    def k(self, j, z, s):
        coef = self.coefs[s == 1 and not 0 <= z < N]
        return self.once(("k", j, z, s), lambda: wide(coef[j, Z0 + z, s]))

    def x_neighbour(self, field, c, z, s, n):
        shift, edge = (x_up, self.top) if field == "e" else (x_down, self.bottom)

        def moved(half):
            return self.once(("x", field, c, z, half, n), lambda: shift(self.get(field, c, z, half, n)))

        kinds = ("xeh", "xe") if field == "e" else ("xhl", "xh")
        from_block = self.source(x_source(kinds[s], n, c - 1, z))
        return choose(edge, add(moved(1 - s), from_block), moved(s))

    def y_neighbour(self, field, c, z, s, n):
        shift = y_ahead if field == "e" else y_behind
        return self.once(("y", field, c, z, s, n), lambda: shift(self.get(field, c, z, s, n)))

    def z_neighbour(self, field, c, z, s, n):
        kind, at = ("ze", z + 1) if field == "e" else ("zh", z - 1)
        return add(self.get(field, c, at, s, n), self.source(z_source(kind, n, c, at, s)))

    def step_h(self, n, c, z, s):
        m = n - 1
        ex, ey, ez = (lambda c=c: self.get("e", c, z, s, m) for c in range(3))
        if c == 0:
            curl = sub(sub(self.y_neighbour("e", 2, z, s, m), ez()), sub(self.z_neighbour("e", 1, z, s, m), ey()))
        elif c == 1:
            curl = sub(sub(self.z_neighbour("e", 0, z, s, m), ex()), sub(self.x_neighbour("e", 2, z, s, m), ez()))
        else:
            curl = sub(sub(self.x_neighbour("e", 1, z, s, m), ey()), sub(self.y_neighbour("e", 0, z, s, m), ex()))
        value = sub(mul(self.k(0, z, s), self.get("h", c, z, s, m)), mul(self.k(1, z, s), curl))
        self.put("h", c, z, s, n, value)

    def step_e(self, n, c, z, s):
        hx, hy, hz = (lambda c=c: self.get("h", c, z, s, n) for c in range(3))
        if c == 0:
            curl = sub(sub(hz(), self.y_neighbour("h", 2, z, s, n)), sub(hy(), self.z_neighbour("h", 1, z, s, n)))
        elif c == 1:
            curl = sub(sub(hx(), self.z_neighbour("h", 0, z, s, n)), sub(hz(), self.x_neighbour("h", 2, z, s, n)))
        else:
            curl = sub(sub(hy(), self.x_neighbour("h", 1, z, s, n)), sub(hx(), self.y_neighbour("h", 0, z, s, n)))
        old, new = (n - 1) % 2, n % 2
        k = [self.k(j, z, s) for j in range(5)]
        e_new, p_new = e_update(
            curl, self.get("e", c, z, s, n - 1), self.get(old, c, z, s, n), self.get(new, c, z, s, n), k, self.polar
        )
        self.put("e", c, z, s, n, e_new)
        if n < STEPS or s == 0:
            self.put(new, c, z, s, n, p_new)

    def row(self, n, z, seen, field):
        step = self.step_h if field == "h" else self.step_e
        for s in range(2):
            for c in range(3):
                if (c, z, s) in NEED[(field, n)] and ((c, z, s) in LATE[(field, n)]) == self.second:
                    step(n, c, z, s)
                    if field == "e" and (z, s) == (N // 2, 0):
                        seen[n - 1, c] = self.get("e", c, z, s, n)
        self.memo = {}


def near_kernel(
    live, e_hbm, h_hbm, p_hbm, coef_in, tables, high, low, ghosts, g1, g0, weights,
    e, h, a, b, coef, own, seen, tiles,
    side, sems,
):
    above_first = lax.rem(lax.axis_index("grp"), 2) == 0
    mine = pl.ds(Z0, N)
    large = start_all(
        [
            (e_hbm, e.at[:, mine, 0]),
            (h_hbm, h.at[:, mine, 0]),
            (p_hbm.at[0], a.at[:, mine, 0]),
            (p_hbm.at[1], b.at[:, mine, 0]),
        ],
        sems,
    )
    for i in range(2 * FREQS * STEPS):
        tiles[i] = jnp.broadcast_to(weights[0:1, i : i + 1], (N, LANES))
    for i in range(OWN_TILES):
        x, y = g0[i], g1[i]
        own[0, i] = jnp.where(above_first, x, y)
        own[1, i] = jnp.where(above_first, y, x)
    ghost_materials(side, [(high, HX, HIGH), (low, LX, LOW)])
    columns = [(z, 1, side[...], z) for z in range(N)]
    columns += [(z, 0, own[1 if z < 0 else 0, 8, :, 0:LANES], z % N) for z in (*range(-4, 0), *range(N, N + 3))]
    fill_coefficients(coef, columns, tables)
    for z in range(N):
        for j in range(5):
            coef[j, Z0 + z, 0] = coef_in[j, z]
    polar = [wide(tables[16 + j]) for j in range(3)]
    wait_all(large[:2])
    live.update({(field, c, z, 0): 0 for field in FIELDS for c in range(3) for z in range(N)})
    places = {"own": own, "high": high, "low": low, "ghosts": ghosts}
    run = Pass(False, live, [(e, h, a, b)] * 2, [coef, None], polar, places, sublane((N, NY)))
    for n in range(1, STEPS + 1):
        for z in range(-4, N + 3):
            run.row(n, z, seen, "h")
        if n == 1:
            wait_all(large[2:])
        for z in range(-4, N + 3):
            run.row(n, z, seen, "e")


def ghost_materials(tile, found):
    tile[...] = jnp.zeros((N, LANES), jnp.float32)
    for source, table, places in found:
        for x in places:
            t, r = table[("mat", 0, 0, x)]
            tile[x : x + 1, :] = source[t, r : r + 1, 0:LANES]


def fill_coefficients(coef, columns, tables):
    stacked = [[tables[4 * k + j] for j in range(4)] for k in range(4)]
    for z, s, tile, at in columns:
        kind = jnp.broadcast_to(tile[:, at : at + 1], (N, LANES))
        for j, v in enumerate(row_coefficients(kind, stacked)):
            coef[j, Z0 + z, s] = v


def far_kernel(
    live, e_in, h_in, a_in, b_in, coef_in, own, seen_in, tables, high, low, ghosts, f1, f0, weights,
    e_out, h_out, p_out, s_out,
    e, h, a, b, coef, seen, far, corners, spectrum, sems,
):
    above_first = lax.rem(lax.axis_index("grp"), 2) == 0
    for i in range(FAR_TILES):
        x, y = f0[i], f1[i]
        far[0, i] = jnp.where(above_first, x, y)
        far[1, i] = jnp.where(above_first, y, x)
    for i, table in enumerate((HF, LF)):
        ghost_materials(corners.at[i], [(far.at[i], table, HIGH + LOW)])
    columns = [(z, 1, corners[1 if z < 0 else 0], z % N) for z in (*range(-4, 0), *range(N, N + 3))]
    fill_coefficients(coef, columns, tables)
    polar = [wide(tables[16 + j]) for j in range(3)]
    places = {"own": own, "far": far, "high": high, "low": low, "ghosts": ghosts}
    run = Pass(True, live, [(e_in, h_in, a_in, b_in), (e, h, a, b)], [coef_in, coef], polar, places, sublane((N, NY)))
    for field, n, last, made in ((0, STEPS, a, a_in), (1, STEPS - 1, b, b_in), ("e", STEPS, e, e_in), ("h", STEPS, h, h_in)):
        for c in range(3):
            for z in range(N):
                if (c, z, 0) not in LATE[("h" if field == "h" else "e", n)]:
                    last[c, Z0 + z, 0] = made[c, Z0 + z, 0]
    outs = []
    for n in range(1, STEPS + 1):
        if n == STEPS:
            outs += start_all([(b.at[:, pl.ds(Z0, N), 0], p_out.at[1])], sems.at[pl.ds(1, 1)])
        for z in range(-4, N + 3):
            run.row(n, z, seen, "h")
        if n == STEPS:
            outs += start_all([(h.at[:, pl.ds(Z0, N), 0], h_out)], sems.at[pl.ds(0, 1)])
            order = [*range(N // 2, N), *range(N // 2)]
        else:
            order = range(-4, N + 3)
        for z in order:
            run.row(n, z, seen, "e")
            if n == STEPS:
                if z % 4 == 3:
                    at, to = pl.ds(Z0 + z - 3, 4), pl.ds(z - 3, 4)
                    outs += start_all(
                        [(e.at[:, at, 0], e_out.at[:, to]), (a.at[:, at, 0], p_out.at[0, :, to])],
                        sems.at[pl.ds(3 + z // 4 * 2, 2)],
                    )
                if z == N // 2:
                    for c in range(3):
                        planes = [
                            (seen if (c, z, 0) in LATE[("e", i + 1)] else seen_in)[i, c] for i in range(STEPS)
                        ]
                        for f in range(FREQS):
                            for q in range(2):
                                total = wide(weights[2 * f + q]) * planes[0]
                                for i in range(1, STEPS):
                                    total = total + wide(weights[2 * FREQS * i + 2 * f + q]) * planes[i]
                                spectrum[f, q, c, 0] = total
                    outs += start_all([(spectrum, s_out)], sems.at[pl.ds(2, 1)])
    wait_all(outs)


HBM = pl.BlockSpec(memory_space=pltpu.HBM)
VMEM = pl.BlockSpec(memory_space=pltpu.VMEM)
SMEM = pl.BlockSpec(memory_space=pltpu.SMEM)


def f32(*shape):
    return jax.ShapeDtypeStruct(shape, jnp.float32)


def vmem(*shape):
    return pltpu.VMEM(shape, jnp.float32)


def small_tables():
    return [pltpu.SMEM((N, N), jnp.int32), pltpu.SMEM((4,), jnp.float32), pltpu.SMEM((4,), jnp.float32), pltpu.SMEM((3,), jnp.float32)]


def params():
    return pltpu.CompilerParams(vmem_limit_bytes=32 * 1024 * 1024)


def swap(block, axis, parity):
    size = lax.axis_size(axis)
    route = []
    for i in range(parity, size - 1, 2):
        route += [(i, i + 1), (i + 1, i)]
    return lax.ppermute(block, axis, route)


def call_alone(inputs):
    plane = (2 * STEPS, N, NY)
    return pl.pallas_call(
        alone_kernel,
        out_shape=[f32(X_TILES, N, NY)] * 2 + [f32(OWN_TILES, N, NY)] * 2 + [f32(5, N, N, LANES), f32(19, N, LANES)],
        in_specs=[HBM] * 7,
        out_specs=[VMEM] * 6,
        scratch_shapes=[vmem(3, N, N, NY)] * 4
        + [vmem(*plane)] * 4
        + [vmem(4, 4, N, NY)]
        + small_tables()
        + [pltpu.SemaphoreType.DMA((8,))],
        compiler_params=params(),
        name="alone",
    )(*inputs)


def call_forward(r1, r0):
    return pl.pallas_call(
        forward_kernel,
        out_shape=[f32(FAR_TILES, N, NY)] * 2 + [f32(X_TILES, N, NY)] * 2 + [f32(7, N, NY)],
        in_specs=[VMEM] * 2,
        out_specs=[VMEM] * 5,
        scratch_shapes=[vmem(2, FAR_TILES, N, NY)],
        compiler_params=params(),
        name="forward",
    )(r1, r0)


def call_near(live, fields, coef, tables, received, weights):
    state = f32(3, ROWS, 2, N, NY)
    return pl.pallas_call(
        functools.partial(near_kernel, live),
        out_shape=[state] * 4
        + [f32(5, ROWS, 2, N, LANES), f32(2, OWN_TILES, N, NY), f32(STEPS, 3, N, NY)]
        + [f32(2 * FREQS * STEPS, N, LANES)],
        in_specs=[HBM] * 3 + [VMEM] * 8,
        out_specs=[VMEM] * 8,
        scratch_shapes=[vmem(N, LANES), pltpu.SemaphoreType.DMA((4,))],
        compiler_params=params(),
        cost_estimate=pl.CostEstimate(flops=20_000_000, bytes_accessed=20_000_000, transcendentals=0),
        name="near",
    )(*fields, coef, tables, *received, weights)


def call_far(live, state, tables, received, weights):
    return pl.pallas_call(
        functools.partial(far_kernel, live),
        out_shape=[f32(3, N, N, NY), f32(3, N, N, NY), f32(2, 3, N, N, NY), f32(FREQS, 2, 3, 1, N, NY)],
        in_specs=[VMEM] * 14,
        out_specs=[HBM] * 4,
        scratch_shapes=[vmem(3, ROWS, 2, N, NY)] * 4
        + [
            vmem(5, ROWS, 2, N, LANES),
            vmem(STEPS, 3, N, NY),
            vmem(2, FAR_TILES, N, NY),
            vmem(2, N, LANES),
            vmem(FREQS, 2, 3, 1, N, NY),
            pltpu.SemaphoreType.DMA((7,)),
        ],
        compiler_params=params(),
        name="far",
    )(*state, tables, *received, weights)


def on_device(e_field, h_field, polar, material, eps_table, loss_table, lorentz, freqs):
    inputs = (e_field, h_field, polar, material, eps_table, loss_table, lorentz)
    inputs = tuple(pltpu.with_memory_space_constraint(x, pltpu.HBM) for x in inputs)
    m0, m1, w0, w1, coef, tables = call_alone(inputs)
    r1 = swap(m1, "dev", 1)
    r0 = swap(m0, "dev", 0)
    g1 = swap(w1, "grp", 1)
    g0 = swap(w0, "grp", 0)
    v1, v0, high, low, ghosts = call_forward(r1, r0)
    f1 = swap(v1, "grp", 1)
    f0 = swap(v0, "grp", 0)
    angles = freqs * jnp.arange(1, STEPS + 1, dtype=jnp.float32)[:, None]
    weights = jnp.stack([jnp.cos(angles), -jnp.sin(angles)], axis=2)
    weights = weights.reshape(1, 2 * FREQS * STEPS)
    live = {}
    *state, weights = call_near(live, inputs[:3], coef, tables, (high, low, ghosts, g1, g0), weights)
    return tuple(call_far(live, state, tables, (high, low, ghosts, f1, f0), weights))


def solution(mesh):
    placed = (
        P(None, "grp", "dev", None),
        P(None, "grp", "dev", None),
        P(None, None, "grp", "dev", None),
        P("grp", "dev"),
        P(),
        P(),
        P(),
        P(),
    )
    return jax.shard_map(
        on_device,
        mesh=mesh,
        in_specs=placed,
        out_specs=(
            P(None, "grp", "dev", None),
            P(None, "grp", "dev", None),
            P(None, None, "grp", "dev", None),
            P(None, None, None, "grp", "dev", None),
        ),
        check_vma=False,
    )
```

```python
import functools

import jax
import jax.numpy as jnp
from jax import lax
from jax.experimental import pallas as pl
from jax.experimental.pallas import tpu as pltpu
from jax.sharding import PartitionSpec as P


STEPS = 4
FREQS = 4
COURANT = 0.5
N = 8
NY = 640
LANES = 128

ROWS = 17
Z0 = 5

X_TILES = 12
OWN_TILES = 11
FAR_TILES = 7


def ladder(kind, c, first, count, start, way):
    return [(kind, first + i, c, start + way * j) for i in range(count) for j in range(count - i)]


def materials(places):
    return [("mat", 0, 0, x) for x in places]


def ray_rows(entries, tile, spare=()):
    free = [*spare, *((tile + k // N, k % N) for k in range(len(entries)))]
    return dict(zip(entries, free))


HIGH = (0, 1, 2)
LOW = (4, 5, 6, 7)
HX = ray_rows(
    ladder("ze", 0, 0, 3, 0, 1) + ladder("ze", 1, 0, 3, 0, 1) + ladder("zh", 0, 1, 3, 0, 1) + ladder("zh", 1, 1, 2, 0, 1) + materials(HIGH),
    8,
)
LX = ray_rows(
    ladder("ze", 0, 0, 4, 7, -1) + ladder("ze", 1, 0, 3, 7, -1) + ladder("zh", 0, 1, 3, 7, -1) + ladder("zh", 1, 1, 3, 7, -1) + materials(LOW),
    8,
)
HZ = ray_rows(
    ladder("xe", 0, 0, 3, 0, 1) + ladder("xe", 1, 0, 3, 0, 1) + ladder("xh", 0, 1, 2, 0, 1) + ladder("xh", 1, 1, 2, 0, 1)
    + materials([0]),
    8,
)
LZ = ray_rows(
    ladder("xe", 0, 0, 3, 7, -1) + ladder("xe", 1, 0, 3, 7, -1) + ladder("xh", 0, 1, 3, 7, -1) + ladder("xh", 1, 1, 2, 7, -1)
    + materials([0]),
    8,
)
HF = ray_rows(
    ladder("xhl", 0, 1, 2, 0, 1) + ladder("xhl", 1, 1, 3, 0, 1) + ladder("xeh", 0, 0, 3, 0, 1) + ladder("xeh", 1, 0, 3, 0, 1)
    + materials(HIGH + LOW),
    4,
    ((1, 3), (1, 4), (3, 2), (3, 5)),
)
LF = ray_rows(
    ladder("xhl", 0, 1, 3, 7, -1) + ladder("xhl", 1, 1, 3, 7, -1) + ladder("xeh", 0, 0, 3, 7, -1) + ladder("xeh", 1, 0, 4, 7, -1)
    + materials(HIGH + LOW),
    3,
    ((1, 2), (1, 4), (2, 5)),
)


def ghost_place(kind, n, c, x):
    if kind == "ze":
        return {0: (c, x), 3: (c, (x + 4) % N), 1: (2 + c, x), 2: (2 + c, (x + 4) % N)}[n]
    return {1: (c, x), 3: (c, (x + 4) % N), 2: (2, (x + 4 * c) % N)}[n]


def ghost_tile(ref, kind, n, c):
    tile, row = ghost_place(kind, n, c, 0)
    value = ref[tile]
    return pltpu.roll(value, 4, 0) if row == 4 else value


def slot_e(n, c):
    return 2 * n + c


def slot_h(n, c):
    return 2 * (n - 1) + c


def wide(tile):
    return jnp.concatenate([tile] * (NY // LANES), axis=1)


def sublane(shape):
    return lax.broadcasted_iota(jnp.int32, shape, 0)


def lane(shape):
    return lax.broadcasted_iota(jnp.int32, shape, 1)


def add(x, y):
    return y if x is None else x if y is None else x + y


def sub(x, y):
    return x if y is None else -y if x is None else x - y


def mul(k, x):
    return None if x is None else k * x


def y_ahead(v):
    if v is None:
        return None
    r = pltpu.roll(v, NY - 1, 1)
    last = r[:, NY - LANES :]
    return jnp.concatenate([r[:, : NY - LANES], jnp.where(lane(last.shape) == LANES - 1, 0.0, last)], axis=1)


def y_behind(v):
    if v is None:
        return None
    r = pltpu.roll(v, 1, 1)
    first = r[:, :LANES]
    return jnp.concatenate([jnp.where(lane(first.shape) == 0, 0.0, first), r[:, LANES:]], axis=1)


def x_up(v):
    return None if v is None else pltpu.roll(v, N - 1, 0)


def x_down(v):
    return None if v is None else pltpu.roll(v, 1, 0)


def choose(edge, x, y):
    if x is None and y is None:
        return None
    return jnp.where(edge, 0.0 if x is None else x, 0.0 if y is None else y)


def kind_tables(eps_ref, loss_ref):
    out = []
    for k in range(4):
        damping = jnp.full((N, LANES), loss_ref[k], jnp.float32)
        permittivity = jnp.full((N, LANES), eps_ref[k], jnp.float32)
        scale = 1.0 / (1.0 + damping)
        inverse = 1.0 / permittivity
        out.append(((1.0 - damping) * scale, COURANT * scale, COURANT * scale * inverse, inverse))
    return out


def row_coefficients(kind, tables):
    masks = [kind == k + 1.0 for k in range(4)]
    out = []
    for j in range(4):
        total = jnp.zeros((N, LANES), jnp.float32)
        for k in range(4):
            total = jnp.where(masks[k], tables[k][j], total)
        out.append(total)
    out.append(jnp.where(masks[3], 1.0, 0.0))
    return out


def polar_scalars(lorentz_ref):
    shape = (N, LANES)
    a = jnp.full(shape, lorentz_ref[0], jnp.float32)
    g = jnp.full(shape, lorentz_ref[1], jnp.float32)
    s = jnp.full(shape, lorentz_ref[2], jnp.float32)
    scale = 1.0 / (1.0 + 0.5 * g)
    return (1.0 - a * a - 0.5 * g) * scale, (1.0 - 0.5 * g) * scale, s * a * a * scale, a * a * scale


def own_kinds(material_ref):
    row = sublane((N, LANES))
    out = []
    for z in range(N):
        kind = jnp.zeros((N, LANES), jnp.int32)
        for x in range(N):
            kind = jnp.where(row == x, material_ref[z, x] + 1, kind)
        out.append(kind.astype(jnp.float32))
    return out


def e_update(curl, e, a, b, k, polar):
    retain, _, e_gain, inverse, active = k
    p, q, r = polar
    moved = mul(active, add(sub(mul(p, a), mul(q, b)), mul(r, e)))
    e_new = sub(add(mul(retain, e), mul(e_gain, curl)), mul(inverse, moved))
    p_new = add(a, moved)
    if b is None:
        return e_new, mul(active, p_new)
    return e_new, jnp.where(active > 0.5, p_new, b)


def start_all(pairs, sems):
    copies = [pltpu.make_async_copy(source, target, sems.at[i]) for i, (source, target) in enumerate(pairs)]
    for copy in copies:
        copy.start()
    return copies


def wait_all(copies):
    for copy in copies:
        copy.wait()


def alone_kernel(
    e_hbm, h_hbm, p_hbm, material_hbm, eps_hbm, loss_hbm, lorentz_hbm,
    m0, m1, w0, w1, coef, shared,
    e0, h0, p0, e, h, current, change, change_coef, packed_ref, ze, zh, xe, xh, rays, material, eps, loss, lorentz, sems,
):
    high_first = lax.rem(lax.axis_index("dev"), 2) == 0
    above_first = lax.rem(lax.axis_index("grp"), 2) == 0
    small = start_all(
        [(material_hbm, material), (eps_hbm, eps), (loss_hbm, loss), (lorentz_hbm, lorentz)], sems.at[pl.ds(0, 4)]
    )
    large = start_all(
        [(e_hbm, e0), (h_hbm, h0), (p_hbm, p0)], sems.at[pl.ds(4, 3)]
    )
    wait_all(small)
    tables = kind_tables(eps, loss)
    p, q, r, t = polar_scalars(lorentz)
    for i, v in enumerate([v for table in tables for v in table] + [p, q, r]):
        shared[i] = v
    ln = lane((N, LANES))
    packed = jnp.zeros((N, LANES), jnp.float32)
    line = jnp.zeros((N, LANES), jnp.float32)
    for z, kind in enumerate(own_kinds(material)):
        packed = jnp.where(ln == z, kind, packed)
        line = jnp.where(ln == sublane((N, LANES)) + N * z, kind, line)
        for j, v in enumerate(row_coefficients(kind, tables)):
            coef[j, z] = v
        for j, v in enumerate((q, t, r)):
            change_coef[j, z] = jnp.where(kind == 4.0, v, 0.0)
    packed_ref[...] = packed
    wait_all(large[:2])
    row = sublane((N, NY))
    top = row == N - 1
    bottom = row == 0

    for n in range(1, STEPS + 1):
        e_old, h_old = (e0, h0) if n == 1 else (e, h)
        for c in range(2):
            ze[slot_e(n - 1, c)] = e_old[c, 0]
        for z in range(N):
            retain, h_gain = (wide(coef[j, z]) for j in range(2))
            ex, ey, ez = (e_old[c, z] for c in range(3))
            e1x, e1y = (e_old[c, z + 1] if z < N - 1 else None for c in range(2))
            r = slot_e(n - 1, 0)
            xe[z, r : r + 1, :] = ey[0:1, :]
            xe[z, r + 1 : r + 2, :] = ez[0:1, :]
            xa_y = choose(top, None, x_up(ey))
            xa_z = choose(top, None, x_up(ez))
            hy = retain * h_old[1, z] - h_gain * (sub(e1x, ex) - (xa_z - ez))
            hz = retain * h_old[2, z] - h_gain * ((xa_y - ey) - (y_ahead(ex) - ex))
            h[1, z] = hy
            h[2, z] = hz
            if n < STEPS or z == N - 1:
                h[0, z] = retain * h_old[0, z] - h_gain * ((y_ahead(ez) - ez) - sub(e1y, ey))
            r = slot_h(n, 0)
            xh[z, r : r + 1, :] = hy[N - 1 : N, :]
            xh[z, r + 1 : r + 2, :] = hz[N - 1 : N, :]
        if n == 1:
            wait_all(large[2:])
        for z in range(N if n < STEPS else 0):
            retain, _, e_gain, inverse = (wide(coef[j, z]) for j in range(4))
            q, t, r = (wide(change_coef[j, z]) for j in range(3))
            hx, hy, hz = (h[c, z] for c in range(3))
            lx, ly = (h[c, z - 1] if z else None for c in range(2))
            xb_y = choose(bottom, None, x_down(hy))
            xb_z = choose(bottom, None, x_down(hz))
            curls = (
                (hz - y_behind(hz)) - sub(hy, ly),
                sub(hx, lx) - (hz - xb_z),
                (hy - xb_y) - (hx - y_behind(hx)),
            )
            for c, curl in enumerate(curls):
                if n == 1:
                    cur, dif = p0[0, c, z], p0[0, c, z] - p0[1, c, z]
                else:
                    cur, dif = current[c, z], change[c, z]
                field = e_old[c, z]
                moved = q * dif - t * cur + r * field
                e[c, z] = retain * field + e_gain * curl - inverse * moved
                if n < STEPS - 1:
                    current[c, z] = cur + moved
                    change[c, z] = moved
        for c in range(2):
            zh[slot_h(n, c)] = h[c, N - 1]

    for i, table in enumerate((HX, LX)):
        for (kind, n, c, x), (tile, r) in table.items():
            if kind == "mat":
                rays[i, tile - 8, r : r + 1, 0:LANES] = packed_ref[x : x + 1, :]
                continue
            source = ze.at[slot_e(n, c)] if kind == "ze" else zh.at[slot_h(n, c)]
            rays[i, tile - 8, r : r + 1, :] = source[x : x + 1, :]
    for i, table in enumerate((HZ, LZ)):
        for (kind, n, c, z), (tile, r) in table.items():
            if kind == "mat":
                rays[2 + i, tile - 8, r : r + 1, 0:LANES] = jnp.sum(line, axis=0, keepdims=True)
                continue
            at = slot_e(n, c) if kind == "xe" else slot_h(n, c)
            source = xe if kind == "xe" else xh
            rays[2 + i, tile - 8, r : r + 1, :] = source[z, at : at + 1, :]

    def deal(first, one, other, tile, for_above, for_below):
        one[tile] = jnp.where(first, for_above, for_below)
        other[tile] = jnp.where(first, for_below, for_above)

    for i in range(N):
        deal(high_first, m0, m1, i, xh[i], xe[i])
        deal(above_first, w0, w1, i, zh[i], ze[i])
    for i in range(4):
        deal(high_first, m0, m1, 8 + i, rays[1, i], rays[0, i])
    for i in range(3):
        deal(above_first, w0, w1, 8 + i, rays[3, i], rays[2, i])


def forward_kernel(r1, r0, v1, v0, high, low, ghosts, rays):
    high_first = lax.rem(lax.axis_index("dev"), 2) == 0
    above_first = lax.rem(lax.axis_index("grp"), 2) == 0
    for i in range(X_TILES):
        one, other = r0[i], r1[i]
        high[i] = jnp.where(high_first, one, other)
        low[i] = jnp.where(high_first, other, one)
    for source, table in ((high, HX), (low, LX)):
        for (kind, n, c, x), (tile, r) in table.items():
            value = source[tile, r : r + 1, :]
            if kind == "mat":
                for i, far in enumerate((HF, LF)):
                    to, at = far[(kind, n, c, x)]
                    rays[i, to, at : at + 1, :] = value
            else:
                to, at = ghost_place(kind, n, c, x)
                rays[0 if kind == "ze" else 1, to, at : at + 1, :] = value
    for i, table in enumerate((HF, LF)):
        for (kind, n, c, z), (tile, r) in table.items():
            if kind != "mat":
                at = slot_e(n, c) if kind == "xeh" else slot_h(n, c)
                source = high if kind == "xeh" else low
                rays[i, tile, r : r + 1, :] = source[z, at : at + 1, :]
    for i in range(4):
        ghosts[i] = rays[0, i]
    for i in range(3):
        ghosts[4 + i] = rays[1, i]
    for i in range(FAR_TILES):
        below, above = rays[0, i], rays[1, i]
        v0[i] = jnp.where(above_first, above, below)
        v1[i] = jnp.where(above_first, below, above)


def h_inputs(c, z, s):
    if c == 0:
        return [(2, z, s), (1, z, s), (1, z + 1, s)], [("z", 1)]
    if c == 1:
        return [(0, z, s), (0, z + 1, s), (2, z, s), (2, z, 1 - s)], [("z", 0), ("x", 1)]
    return [(1, z, s), (1, z, 1 - s), (0, z, s)], [("x", 0)]


def e_inputs(c, z, s):
    if c == 0:
        return [(2, z, s), (1, z, s), (1, z - 1, s)], [("z", 1)]
    if c == 1:
        return [(0, z, s), (0, z - 1, s), (2, z, s), (2, z, 1 - s)], [("z", 0), ("x", 1)]
    return [(1, z, s), (1, z, 1 - s), (0, z, s)], [("x", 0)]


def x_source(kind, n, c, z):
    if 0 <= z < N:
        r = slot_e(n, c) if kind == "xeh" else slot_h(n, c)
        return {"xeh": ("high", z, r), "xhl": ("low", z, r)}.get(kind)
    near, far, place = (HZ, HF, z - N) if z >= N else (LZ, LF, z + N)
    for name, table in (("own", near), ("far", far)):
        if (kind, n, c, place) in table:
            return (name, 0 if z >= N else 1, *table[(kind, n, c, place)])
    return None


def z_source(kind, n, c, z, s):
    if s == 0:
        if (kind, z) == ("ze", N):
            return ("own", 0, slot_e(n, c))
        return ("own", 1, slot_h(n, c)) if (kind, z) == ("zh", -1) else None
    if (kind, z) in (("ze", N), ("zh", -1)) and any(k[:3] == (kind, n, c) for k in (*HX, *LX)):
        return ("far", 0 if z == N else 1, kind, n, c)
    if (kind, z) in (("ze", 0), ("zh", N - 1)) and n < STEPS - (kind == "ze") and (kind, n, c) != ("zh", STEPS - 1, 0):
        return ("ghosts", kind, n, c)
    return None


def sources(field, n, z, s, wanted):
    out = []
    for border, c in wanted:
        if field == "h":
            at = x_source("xe" if s else "xeh", n - 1, c, z) if border == "x" else z_source("ze", n - 1, c, z + 1, s)
        else:
            at = x_source("xh" if s else "xhl", n, c, z) if border == "x" else z_source("zh", n, c, z - 1, s)
        out.append(at)
    return [at for at in out if at is not None]


def plan():
    mine = {(c, z, 0) for c in range(3) for z in range(N)}
    need = {("h", STEPS): set(mine), ("e", STEPS): set(mine)}
    for n in range(STEPS, 0, -1):
        for key in need[("e", n)]:
            need[("h", n)] |= set(e_inputs(*key)[0])
        need[("e", n - 1)] = set(need[("e", n)])
        need[("h", n - 1)] = set(need[("h", n)])
        for key in need[("h", n)]:
            need[("e", n - 1)] |= set(h_inputs(*key)[0])
    late = {("e", 0): set(), ("h", 0): set()}
    for n in range(1, STEPS + 1):
        for field, other, inputs, back in (("h", "e", h_inputs, n - 1), ("e", "h", e_inputs, n)):
            late[(field, n)] = set()
            for key in need[(field, n)]:
                before, wanted = inputs(*key)
                c, z, s = key
                if (
                    (s == 1 and not 0 <= z < N)
                    or key in late[(field, n - 1)]
                    or any(k in late[(other, back)] for k in before)
                    or any(at[0] == "far" for at in sources(field, n, z, s, wanted))
                ):
                    late[(field, n)].add(key)
    return need, late


NEED, LATE = plan()
FIELDS = {"e": 0, "h": 1, 0: 2, 1: 3}


class Pass:
    def __init__(self, second, live, stores, coefs, polar, places, row):
        self.second, self.live, self.stores = second, live, stores
        self.coefs, self.polar, self.places = coefs, polar, places
        self.top, self.bottom = row == N - 1, row == 0
        self.memo = {}

    def once(self, key, make):
        if key not in self.memo:
            self.memo[key] = make()
        return self.memo[key]

    def store(self, field, c, z, s, n):
        late = n > 0 and (c, z, s) in LATE[("h" if field == "h" else "e", n)]
        return self.stores[late][FIELDS[field]]

    def get(self, field, c, z, s, n):
        key = (field, c, z, s)
        if self.live.get(key, STEPS + 1) > n:
            return None
        made = n if field in ("e", "h") else n - 1 if (n - 1) % 2 == field else n - 2
        return self.once((*key, n), lambda: self.store(field, c, z, s, made)[c, Z0 + z, s])

    def put(self, field, c, z, s, n, value):
        if value is None:
            return
        self.store(field, c, z, s, n)[c, Z0 + z, s] = value
        self.live.setdefault((field, c, z, s), n)
        self.memo[(field, c, z, s, n)] = value

    def source(self, at):
        if at is None:
            return None
        if at[0] == "ghosts" or len(at) == 5:
            ref = self.places[at[0]] if at[0] == "ghosts" else self.places["far"].at[at[1]]
            kind, n, c = at[-3:]
            if at[0] == "ghosts" and kind == "zh":
                ref = ref.at[pl.ds(4, 3)]
            return ghost_tile(ref, kind, n, c)
        ref = self.places[at[0]]
        if at[0] in ("high", "low"):
            return ref[at[1], at[2] : at[2] + 1, :]
        if len(at) == 3:
            return ref[at[1], at[2]]
        return ref[at[1], at[2], at[3] : at[3] + 1, :]

    def k(self, j, z, s):
        coef = self.coefs[s == 1 and not 0 <= z < N]
        return self.once(("k", j, z, s), lambda: wide(coef[j, Z0 + z, s]))

    def x_neighbour(self, field, c, z, s, n):
        shift, edge = (x_up, self.top) if field == "e" else (x_down, self.bottom)

        def moved(half):
            return self.once(("x", field, c, z, half, n), lambda: shift(self.get(field, c, z, half, n)))

        kinds = ("xeh", "xe") if field == "e" else ("xhl", "xh")
        from_block = self.source(x_source(kinds[s], n, c - 1, z))
        return choose(edge, add(moved(1 - s), from_block), moved(s))

    def y_neighbour(self, field, c, z, s, n):
        shift = y_ahead if field == "e" else y_behind
        return self.once(("y", field, c, z, s, n), lambda: shift(self.get(field, c, z, s, n)))

    def z_neighbour(self, field, c, z, s, n):
        kind, at = ("ze", z + 1) if field == "e" else ("zh", z - 1)
        return add(self.get(field, c, at, s, n), self.source(z_source(kind, n, c, at, s)))

    def step_h(self, n, c, z, s):
        m = n - 1
        ex, ey, ez = (lambda c=c: self.get("e", c, z, s, m) for c in range(3))
        if c == 0:
            curl = sub(sub(self.y_neighbour("e", 2, z, s, m), ez()), sub(self.z_neighbour("e", 1, z, s, m), ey()))
        elif c == 1:
            curl = sub(sub(self.z_neighbour("e", 0, z, s, m), ex()), sub(self.x_neighbour("e", 2, z, s, m), ez()))
        else:
            curl = sub(sub(self.x_neighbour("e", 1, z, s, m), ey()), sub(self.y_neighbour("e", 0, z, s, m), ex()))
        value = sub(mul(self.k(0, z, s), self.get("h", c, z, s, m)), mul(self.k(1, z, s), curl))
        self.put("h", c, z, s, n, value)

    def step_e(self, n, c, z, s):
        hx, hy, hz = (lambda c=c: self.get("h", c, z, s, n) for c in range(3))
        if c == 0:
            curl = sub(sub(hz(), self.y_neighbour("h", 2, z, s, n)), sub(hy(), self.z_neighbour("h", 1, z, s, n)))
        elif c == 1:
            curl = sub(sub(hx(), self.z_neighbour("h", 0, z, s, n)), sub(hz(), self.x_neighbour("h", 2, z, s, n)))
        else:
            curl = sub(sub(hy(), self.x_neighbour("h", 1, z, s, n)), sub(hx(), self.y_neighbour("h", 0, z, s, n)))
        old, new = (n - 1) % 2, n % 2
        k = [self.k(j, z, s) for j in range(5)]
        e_new, p_new = e_update(
            curl, self.get("e", c, z, s, n - 1), self.get(old, c, z, s, n), self.get(new, c, z, s, n), k, self.polar
        )
        self.put("e", c, z, s, n, e_new)
        if n < STEPS or s == 0:
            self.put(new, c, z, s, n, p_new)

    def row(self, n, z, seen, field):
        step = self.step_h if field == "h" else self.step_e
        for s in range(2):
            for c in range(3):
                if (c, z, s) in NEED[(field, n)] and ((c, z, s) in LATE[(field, n)]) == self.second:
                    step(n, c, z, s)
                    if field == "e" and (z, s) == (N // 2, 0):
                        seen[n - 1, c] = self.get("e", c, z, s, n)
        self.memo = {}


def near_kernel(
    live, e_hbm, h_hbm, p_hbm, coef_in, tables, high, low, ghosts, g1, g0, weights,
    e, h, a, b, coef, own, seen, tiles,
    side, sems,
):
    above_first = lax.rem(lax.axis_index("grp"), 2) == 0
    mine = pl.ds(Z0, N)
    large = start_all(
        [
            (e_hbm, e.at[:, mine, 0]),
            (h_hbm, h.at[:, mine, 0]),
            (p_hbm.at[0], a.at[:, mine, 0]),
            (p_hbm.at[1], b.at[:, mine, 0]),
        ],
        sems,
    )
    for i in range(2 * FREQS * STEPS):
        tiles[i] = jnp.broadcast_to(weights[0:1, i : i + 1], (N, LANES))
    for i in range(OWN_TILES):
        x, y = g0[i], g1[i]
        own[0, i] = jnp.where(above_first, x, y)
        own[1, i] = jnp.where(above_first, y, x)
    ghost_materials(side, [(high, HX, HIGH), (low, LX, LOW)])
    columns = [(z, 1, side[...], z) for z in range(N)]
    shape = (N, LANES)
    for z in (*range(-4, 0), *range(N, N + 3)):
        i, (t, r) = (1, LZ[("mat", 0, 0, 0)]) if z < 0 else (0, HZ[("mat", 0, 0, 0)])
        line = jnp.broadcast_to(own[i, t, r : r + 1, 0:LANES], shape)
        here = lane(shape) == sublane(shape) + N * (z % N)
        columns.append((z, 0, jnp.sum(jnp.where(here, line, 0.0), axis=1, keepdims=True), 0))
    fill_coefficients(coef, columns, tables)
    for z in range(N):
        for j in range(5):
            coef[j, Z0 + z, 0] = coef_in[j, z]
    polar = [wide(tables[16 + j]) for j in range(3)]
    wait_all(large[:2])
    live.update({(field, c, z, 0): 0 for field in FIELDS for c in range(3) for z in range(N)})
    places = {"own": own, "high": high, "low": low, "ghosts": ghosts}
    run = Pass(False, live, [(e, h, a, b)] * 2, [coef, None], polar, places, sublane((N, NY)))
    for n in range(1, STEPS + 1):
        for z in range(-4, N + 3):
            run.row(n, z, seen, "h")
        if n == 1:
            wait_all(large[2:])
        for z in range(-4, N + 3):
            run.row(n, z, seen, "e")


def ghost_materials(tile, found):
    tile[...] = jnp.zeros((N, LANES), jnp.float32)
    for source, table, places in found:
        for x in places:
            t, r = table[("mat", 0, 0, x)]
            tile[x : x + 1, :] = source[t, r : r + 1, 0:LANES]


def fill_coefficients(coef, columns, tables):
    stacked = [[tables[4 * k + j] for j in range(4)] for k in range(4)]
    for z, s, tile, at in columns:
        kind = jnp.broadcast_to(tile[:, at : at + 1], (N, LANES))
        for j, v in enumerate(row_coefficients(kind, stacked)):
            coef[j, Z0 + z, s] = v


def far_kernel(
    live, e_in, h_in, a_in, b_in, coef_in, own, seen_in, tables, high, low, ghosts, f1, f0, weights,
    e_out, h_out, p_out, s_out,
    e, h, a, b, coef, seen, far, corners, spectrum, sems,
):
    above_first = lax.rem(lax.axis_index("grp"), 2) == 0
    for i in range(FAR_TILES):
        x, y = f0[i], f1[i]
        far[0, i] = jnp.where(above_first, x, y)
        far[1, i] = jnp.where(above_first, y, x)
    for i, table in enumerate((HF, LF)):
        ghost_materials(corners.at[i], [(far.at[i], table, HIGH + LOW)])
    columns = [(z, 1, corners[1 if z < 0 else 0], z % N) for z in (*range(-4, 0), *range(N, N + 3))]
    fill_coefficients(coef, columns, tables)
    polar = [wide(tables[16 + j]) for j in range(3)]
    places = {"own": own, "far": far, "high": high, "low": low, "ghosts": ghosts}
    run = Pass(True, live, [(e_in, h_in, a_in, b_in), (e, h, a, b)], [coef_in, coef], polar, places, sublane((N, NY)))
    for field, n, last, made in ((0, STEPS, a, a_in), (1, STEPS - 1, b, b_in), ("e", STEPS, e, e_in), ("h", STEPS, h, h_in)):
        for c in range(3):
            for z in range(N):
                if (c, z, 0) not in LATE[("h" if field == "h" else "e", n)]:
                    last[c, Z0 + z, 0] = made[c, Z0 + z, 0]
    outs = []
    for n in range(1, STEPS + 1):
        if n == STEPS:
            outs += start_all([(b.at[:, pl.ds(Z0, N), 0], p_out.at[1])], sems.at[pl.ds(1, 1)])
        for z in range(-4, N + 3):
            run.row(n, z, seen, "h")
        if n == STEPS:
            outs += start_all([(h.at[:, pl.ds(Z0, N), 0], h_out)], sems.at[pl.ds(0, 1)])
            order = [*range(N // 2, N), *range(N // 2)]
        else:
            order = range(-4, N + 3)
        for z in order:
            run.row(n, z, seen, "e")
            if n == STEPS:
                if z % 4 == 3:
                    at, to = pl.ds(Z0 + z - 3, 4), pl.ds(z - 3, 4)
                    outs += start_all(
                        [(e.at[:, at, 0], e_out.at[:, to]), (a.at[:, at, 0], p_out.at[0, :, to])],
                        sems.at[pl.ds(3 + z // 4 * 2, 2)],
                    )
                if z == N // 2:
                    for c in range(3):
                        planes = [
                            (seen if (c, z, 0) in LATE[("e", i + 1)] else seen_in)[i, c] for i in range(STEPS)
                        ]
                        for f in range(FREQS):
                            for q in range(2):
                                total = wide(weights[2 * f + q]) * planes[0]
                                for i in range(1, STEPS):
                                    total = total + wide(weights[2 * FREQS * i + 2 * f + q]) * planes[i]
                                spectrum[f, q, c, 0] = total
                    outs += start_all([(spectrum, s_out)], sems.at[pl.ds(2, 1)])
    wait_all(outs)


HBM = pl.BlockSpec(memory_space=pltpu.HBM)
VMEM = pl.BlockSpec(memory_space=pltpu.VMEM)
SMEM = pl.BlockSpec(memory_space=pltpu.SMEM)


def f32(*shape):
    return jax.ShapeDtypeStruct(shape, jnp.float32)


def vmem(*shape):
    return pltpu.VMEM(shape, jnp.float32)


def small_tables():
    return [pltpu.SMEM((N, N), jnp.int32), pltpu.SMEM((4,), jnp.float32), pltpu.SMEM((4,), jnp.float32), pltpu.SMEM((3,), jnp.float32)]


def params():
    return pltpu.CompilerParams(vmem_limit_bytes=32 * 1024 * 1024)


def swap(block, axis, parity):
    size = lax.axis_size(axis)
    route = []
    for i in range(parity, size - 1, 2):
        route += [(i, i + 1), (i + 1, i)]
    return lax.ppermute(block, axis, route)


def call_alone(inputs):
    plane = (2 * STEPS, N, NY)
    return pl.pallas_call(
        alone_kernel,
        out_shape=[f32(X_TILES, N, NY)] * 2 + [f32(OWN_TILES, N, NY)] * 2 + [f32(5, N, N, LANES), f32(19, N, LANES)],
        in_specs=[HBM] * 7,
        out_specs=[VMEM] * 6,
        scratch_shapes=[vmem(3, N, N, NY), vmem(3, N, N, NY), vmem(2, 3, N, N, NY)]
        + [vmem(3, N, N, NY)] * 4
        + [vmem(3, N, N, LANES), vmem(N, LANES)]
        + [vmem(*plane)] * 4
        + [vmem(4, 4, N, NY)]
        + small_tables()
        + [pltpu.SemaphoreType.DMA((7,))],
        compiler_params=params(),
        name="alone",
    )(*inputs)


def call_forward(r1, r0):
    return pl.pallas_call(
        forward_kernel,
        out_shape=[f32(FAR_TILES, N, NY)] * 2 + [f32(X_TILES, N, NY)] * 2 + [f32(7, N, NY)],
        in_specs=[VMEM] * 2,
        out_specs=[VMEM] * 5,
        scratch_shapes=[vmem(2, FAR_TILES, N, NY)],
        compiler_params=params(),
        name="forward",
    )(r1, r0)


def call_near(live, fields, coef, tables, received, weights):
    state = f32(3, ROWS, 2, N, NY)
    return pl.pallas_call(
        functools.partial(near_kernel, live),
        out_shape=[state] * 4
        + [f32(5, ROWS, 2, N, LANES), f32(2, OWN_TILES, N, NY), f32(STEPS, 3, N, NY)]
        + [f32(2 * FREQS * STEPS, N, LANES)],
        in_specs=[HBM] * 3 + [VMEM] * 8,
        out_specs=[VMEM] * 8,
        scratch_shapes=[vmem(N, LANES), pltpu.SemaphoreType.DMA((4,))],
        compiler_params=params(),
        cost_estimate=pl.CostEstimate(flops=20_000_000, bytes_accessed=20_000_000, transcendentals=0),
        name="near",
    )(*fields, coef, tables, *received, weights)


def call_far(live, state, tables, received, weights):
    return pl.pallas_call(
        functools.partial(far_kernel, live),
        out_shape=[f32(3, N, N, NY), f32(3, N, N, NY), f32(2, 3, N, N, NY), f32(FREQS, 2, 3, 1, N, NY)],
        in_specs=[VMEM] * 14,
        out_specs=[HBM] * 4,
        scratch_shapes=[vmem(3, ROWS, 2, N, NY)] * 4
        + [
            vmem(5, ROWS, 2, N, LANES),
            vmem(STEPS, 3, N, NY),
            vmem(2, FAR_TILES, N, NY),
            vmem(2, N, LANES),
            vmem(FREQS, 2, 3, 1, N, NY),
            pltpu.SemaphoreType.DMA((7,)),
        ],
        compiler_params=params(),
        name="far",
    )(*state, tables, *received, weights)


def on_device(e_field, h_field, polar, material, eps_table, loss_table, lorentz, freqs):
    inputs = (e_field, h_field, polar, material, eps_table, loss_table, lorentz)
    inputs = tuple(pltpu.with_memory_space_constraint(x, pltpu.HBM) for x in inputs)
    m0, m1, w0, w1, coef, tables = call_alone(inputs)
    r1 = swap(m1, "dev", 1)
    r0 = swap(m0, "dev", 0)
    g1 = swap(w1, "grp", 1)
    g0 = swap(w0, "grp", 0)
    v1, v0, high, low, ghosts = call_forward(r1, r0)
    f1 = swap(v1, "grp", 1)
    f0 = swap(v0, "grp", 0)
    angles = freqs * jnp.arange(1, STEPS + 1, dtype=jnp.float32)[:, None]
    weights = jnp.stack([jnp.cos(angles), -jnp.sin(angles)], axis=2)
    weights = weights.reshape(1, 2 * FREQS * STEPS)
    live = {}
    *state, weights = call_near(live, inputs[:3], coef, tables, (high, low, ghosts, g1, g0), weights)
    return tuple(call_far(live, state, tables, (high, low, ghosts, f1, f0), weights))


def solution(mesh):
    placed = (
        P(None, "grp", "dev", None),
        P(None, "grp", "dev", None),
        P(None, None, "grp", "dev", None),
        P("grp", "dev"),
        P(),
        P(),
        P(),
        P(),
    )
    return jax.shard_map(
        on_device,
        mesh=mesh,
        in_specs=placed,
        out_specs=(
            P(None, "grp", "dev", None),
            P(None, "grp", "dev", None),
            P(None, None, "grp", "dev", None),
            P(None, None, None, "grp", "dev", None),
        ),
        check_vma=False,
    )
```
